256 devices in a mesh: mem: 8 (over z_hi, core), patch: 32 (over z_lo, y, x).
Axes of the slice: x: 4, y: 4, z: 8 (z_hi: 4, z_lo: 2; z = z_hi * 2 + z_lo), core: 2. Of those that a mesh axis runs over, the one named last changes fastest.
Arguments:
- ensemble: float32 [8, 2, 55, 65536], P('mem', None, None, 'patch'), may hold values from -6 to 6
- field: float32 [2, 55, 65536], P(None, None, 'patch'), may hold values from -12 to 12
- diffusivity: float32 [65536], P('patch'), may hold values from 0.08 to 0.16
- neighbours: int32 [7, 65536], P(None, 'patch'), may hold values from 0 to 65535, as said below
- vertical_root: float32 [55, 55], replicated, may hold values from -3 to 3
Outputs:
- covariance_product: float32 [2, 55, 65536], P(None, None, 'patch')
- quadratic: float32 [], replicated
The draws below stay inside these ranges and needn't reach their ends.
Inputs may be any that keep to these rules, and one draw needn't show every extreme that they name: Each neighbours[s, i] is a cell fewer than 128 positions from i in the cyclic order of the 65536 cells, or i itself in unused slots; the relation is symmetric, and no cell other than i appears twice among i's slots.
All inputs are finite; a program needn't handle non-finite values.
Results may differ from the reference program's by a relative error of at most 0.00011.
Values sent between devices are 32-bit elements; how exact they have to be, the bound alone decides.
No kernel may reach another device: no remote copies, remote signals or barrier semaphores. Data moves between devices by JAX's collectives and lax.ppermute only.
A program may use at most 192 MiB of HBM per device.

```python
import math
import jax
import jax.numpy as jnp
from jax import lax

VARS = 2
LEVELS = 55
STEPS = 4
ROW = 128
MEMBERS = 8
NCELLS = 65536


def draw_field(key, part):
    key = jax.random.fold_in(key, 5)
    ramp = 1.0 + 2.0 * jnp.arange(NCELLS, dtype=jnp.float32) / NCELLS
    values = jnp.clip(jax.random.normal(key, (VARS, LEVELS, NCELLS), jnp.float32), -4.0, 4.0)
    return (values * ramp[None, None, :]).astype(jnp.float32)


def pair_cells(key, cells):
    key_shift, key_order, key_keep = jax.random.split(key, 3)
    windows = NCELLS // ROW
    shift = jax.random.randint(key_shift, (), ROW // 4, 3 * ROW // 4 + 1).astype(jnp.int32)
    scores = jax.random.randint(key_order, (windows, ROW), 0, 1 << 20) * ROW + jnp.arange(ROW, dtype=jnp.int32)[None, :]
    order = jnp.argsort(scores, axis=1).astype(jnp.int32)
    rank = jnp.argsort(order, axis=1).astype(jnp.int32)
    mate = jnp.take_along_axis(order, jnp.bitwise_xor(rank, 1), axis=1)
    base = (jnp.arange(windows, dtype=jnp.int32) * ROW)[:, None]
    mate_flat = (base + mate).reshape(NCELLS).astype(jnp.int32)
    shifted = jnp.mod(cells - shift, NCELLS).astype(jnp.int32)
    partner = jnp.mod(jnp.take(mate_flat, shifted) + shift, NCELLS).astype(jnp.int32)
    keep = jax.random.randint(key_keep, (NCELLS,), 0, 10) > 0
    keep_pair = jnp.take(keep, jnp.minimum(cells, partner))
    return jnp.where(keep_pair, partner, cells).astype(jnp.int32)


def draw_neighbours(key, part):
    key = jax.random.fold_in(key, 11)
    key_order = jax.random.fold_in(key, 99)
    cells = jnp.arange(NCELLS, dtype=jnp.int32)
    slots = []
    for which in range(6):
        partner = pair_cells(jax.random.fold_in(key, 100 + which), cells)
        for earlier in slots:
            partner = jnp.where(partner == earlier, cells, partner).astype(jnp.int32)
        slots.append(partner)
    slots.append(cells)
    stacked = jnp.stack(slots, axis=0)
    scores = jax.random.randint(key_order, (7, NCELLS), 0, 1 << 20) * 8 + jnp.arange(7, dtype=jnp.int32)[:, None]
    order = jnp.argsort(scores, axis=0)
    return jnp.take_along_axis(stacked, order, axis=0).astype(jnp.int32)


def draw_vertical_root(key, part):
    key = jax.random.fold_in(key, 7)
    noise = jnp.clip(jax.random.normal(key, (LEVELS, LEVELS), jnp.float32), -4.0, 4.0) * 0.6
    return (jnp.eye(LEVELS, dtype=jnp.float32) + noise / jnp.sqrt(jnp.float32(LEVELS))).astype(jnp.float32)


def block_levels(key, shape, cuts, low, top_value):
    loudness, own = 1.0, jax.random.fold_in(key, 6)
    for position, blocks in cuts:
        draws = jnp.exp(jax.random.uniform(jax.random.fold_in(own, position), (blocks,), jnp.float32, low / len(cuts), top_value / len(cuts)))
        loudness = loudness * jnp.repeat(draws, shape[position] // blocks).reshape([-1 if axis == position else 1 for axis in range(len(shape))])
    return loudness


def scatter_about(stream_key, shape, scale, most, pieces=(), held_as=jnp.bfloat16):
    drawn = scale * jax.random.normal(stream_key, shape, jnp.float32)
    if pieces:
        drawn = drawn * block_levels(stream_key, shape, pieces, -0.22, 0.18)
    return jnp.clip(drawn, -most, most).astype(held_as)


def setup_inputs(seed: int = 0) -> dict:
    key_list = jax.random.split(jax.random.key(seed), 6)
    ensemble = scatter_about(key_list[0], (MEMBERS, VARS, LEVELS, NCELLS), 1.0, 6.0, ((0, 8), (3, 32)), jnp.float32)
    field = draw_field(jax.random.fold_in(key_list[5], 71), 0)
    diffusivity = jnp.clip(jnp.exp(math.log(0.16) - 0.6931472 * jax.random.uniform(key_list[2], (NCELLS,), jnp.float32) ** block_levels(key_list[2], (NCELLS,), ((0, 32),), -0.2, 0.2)), 0.08, 0.16)
    neighbours = draw_neighbours(jax.random.fold_in(key_list[5], 71), 0)
    vertical_root = draw_vertical_root(jax.random.fold_in(key_list[5], 71), 0)
    return {"ensemble": ensemble, "field": field, "diffusivity": diffusivity, "neighbours": neighbours, "vertical_root": vertical_root}


def smooth_once(state, rates, neighbours):
    change = jnp.zeros_like(state)
    for slot in range(7):
        change = change + rates[slot][None, :] * (jnp.take(state, neighbours[slot], axis=1) - state)
    return state + change


def reference(ensemble, field, diffusivity, neighbours, vertical_root):
    rates = 0.5 * (diffusivity[None, :] + jnp.take(diffusivity, neighbours, axis=0))
    total = jnp.zeros(field.shape, jnp.float32)
    for member in range(MEMBERS):
        weighted = ensemble[member, 0] * field[0] + ensemble[member, 1] * field[1]
        spread = weighted
        for repeat in range(STEPS):
            spread = smooth_once(spread, rates, neighbours)
        lowered = jnp.einsum("lk,lc->kc", vertical_root, spread, precision=lax.Precision.HIGHEST)
        raised = jnp.einsum("kl,lc->kc", vertical_root, lowered, precision=lax.Precision.HIGHEST)
        smoothed = raised
        for repeat in range(STEPS):
            smoothed = smooth_once(smoothed, rates, neighbours)
        total = total + ensemble[member] * smoothed[None]
    covariance_product = total / (MEMBERS - 1.0)
    quadratic = jnp.sum(field * covariance_product) / (VARS * LEVELS * NCELLS)
    return covariance_product, quadratic
```

```python
import functools

import jax
import jax.numpy as jnp
from jax import lax
from jax.experimental import pallas as pl
from jax.experimental.pallas import tpu as pltpu
from jax.sharding import PartitionSpec as P

STEPS = 8
REACH = 128
BLOCK = 256
HALO = STEPS * REACH
LEVELS = 55
LANES = 128


def prepare_kernel(
    all_cells, place, ens, field, diff, neigh, head, tail, ens_in, field_in, diff_in, neigh_in, sems
):
    own = diff.shape[1]
    tiles = own // LANES
    half = own // 2
    start = place[0]
    levels = (0, 16, 32, 48, LEVELS)
    copies = []
    for turn in range(4):
        rows = pl.ds(levels[turn] * 2 * tiles, (levels[turn + 1] - levels[turn]) * 2 * tiles)
        copies.append((
            pltpu.make_async_copy(ens.at[rows], ens_in.at[rows], sems.at[0, turn]),
            pltpu.make_async_copy(field.at[rows], field_in.at[rows], sems.at[1, turn]),
        ))
    others = (
        pltpu.make_async_copy(neigh, neigh_in, sems.at[2, 0]),
        pltpu.make_async_copy(diff, diff_in, sems.at[2, 1]),
    )
    for copy in others + copies[0] + copies[1] + copies[2] + copies[3]:
        copy.start()
    for copy in others:
        copy.wait()
    for part, out in ((0, head), (1, tail)):
        cols = pl.ds(part * half, half)
        out[55:56, :] = jnp.ones((1, half), jnp.float32)
        cell = lax.broadcasted_iota(jnp.int32, (7, half), 1) + (start + part * half)
        shift = neigh_in[:, cols] - cell
        shift = jnp.where(shift > all_cells // 2, shift - all_cells, shift)
        shift = jnp.where(shift < -(all_cells // 2), shift + all_cells, shift)
        out[56:63, :] = shift.astype(jnp.float32)
        out[63:64, :] = diff_in[:, cols]
    for turn in range(4):
        for copy in copies[turn]:
            copy.wait()
        low, high = levels[turn], levels[turn + 1]
        rows = pl.ds(low * 2 * tiles, (high - low) * 2 * tiles)
        ens_in[rows, :] = ens_in[rows, :] * field_in[rows, :]
        for part, out in ((0, head), (1, tail)):
            for tile in range(tiles // 2):
                at = low * 2 * tiles + 2 * (part * (tiles // 2) + tile)
                out[low:high, tile * LANES : (tile + 1) * LANES] = (
                    ens_in[pl.ds(at, high - low, stride=2 * tiles), :]
                    + ens_in[pl.ds(at + 1, high - low, stride=2 * tiles), :]
                )


def build_block(shift, store):
    row = lax.broadcasted_iota(jnp.int32, (LANES, LANES), 0).astype(jnp.float32).astype(jnp.bfloat16)
    lane = lax.broadcasted_iota(jnp.int32, (1, LANES), 1).astype(jnp.float32)
    one = jnp.ones((LANES, LANES), jnp.bfloat16)
    zero = jnp.zeros((LANES, LANES), jnp.bfloat16)
    for chunk in range(BLOCK // LANES):
        part = shift[:, chunk * LANES : (chunk + 1) * LANES]
        for side in range(3):
            local = part + (lane + (1.0 - side) * LANES)
            inside = jnp.logical_and(jnp.logical_and(local >= 0.0, local < LANES), part != 0.0)
            local = jnp.where(inside, local, -1.0).astype(jnp.bfloat16)
            hit = zero
            for slot in range(7):
                hit = jnp.where(row == local[slot : slot + 1, :], one, hit)
            store(chunk + side, chunk, hit)
        store((chunk + 3) % 4, chunk, zero)


def split(value, coeff):
    both = jnp.concatenate([value, coeff * value], axis=0)
    high = both.astype(jnp.bfloat16)
    low = (both - high.astype(jnp.float32)).astype(jnp.bfloat16)
    return high, low


def store_parts(buf, at, parts):
    width = parts[0].shape[1]
    buf[0:112, at : at + width] = parts[0]
    buf[112:224, at : at + width] = parts[1]


def sweep(state, now, later, margin, places):
    def matmul(at, width, matrix):
        window = now[:, at + margin - REACH : at + margin + width + REACH]
        return jnp.dot(window, matrix, preferred_element_type=jnp.float32)

    def finish(at, width, kept, total):
        coeff = state[56:57, at : at + width]
        value = state[0:56, at : at + width]
        change = coeff * (total[0:56] + total[112:168]) + (total[56:112] + total[168:224])
        value = value * (1.0 - change[55:56]) + change
        if kept:
            state[0:56, at : at + width] = value
        if later is not None:
            store_parts(later, at + margin, split(value, coeff))

    waiting = None
    for at, width, matrix, kept in places:
        total = matmul(at, width, matrix())
        if waiting is not None:
            finish(*waiting)
        waiting = (at, width, kept, total)
    finish(*waiting)


def interior_blocks(step, count):
    skip = (step + 1) // 2
    return range(skip, count - skip)


def interior_kernel(head, tail, adj, state, buf0, buf1, buf2, buf3):
    bufs = (buf0, buf1, buf2, buf3)
    blocks = adj.shape[0]
    half = blocks // 2
    for block in range(blocks):
        source, at = (head, block * BLOCK) if block < half else (tail, (block - half) * BLOCK)

        def store(down, across, value):
            adj[block, down * LANES : (down + 1) * LANES, across * LANES : (across + 1) * LANES] = value

        value = source[:, at : at + BLOCK]
        build_block(value[56:63], store)
        coeff = 0.5 * value[63:64]
        here = block * BLOCK
        state[0:56, here : here + BLOCK] = value[0:56]
        state[56:64, here : here + BLOCK] = jnp.broadcast_to(coeff, (8, BLOCK))
        store_parts(buf0, here, split(value[0:56], coeff))
    for step in range(1, STEPS - 1):
        whole = interior_blocks(step, blocks)
        places = [(block * BLOCK, BLOCK, functools.partial(lambda b: adj[b], block), True) for block in whole]
        if step % 2:
            low, high = whole[0] - 1, whole[-1] + 1
            places.append((low * BLOCK + REACH, REACH, lambda: adj[low, REACH:, REACH:], False))
            places.append((high * BLOCK, REACH, lambda: adj[high, : BLOCK + REACH, :REACH], False))
        sweep(state, bufs[(step - 1) % 4], bufs[step % 4], 0, places)


def smooth_kernel(
    ids, left, head, tail, right, root, ens, inner, done, own0, own1, own2, own3,
    keep, send, state, outer, buf0, buf1, buf2, buf3, square, rowed,
):
    wide = state.shape[1]
    own = wide - 2 * HALO
    tiles = own // LANES
    blocks = wide // BLOCK
    fringe = HALO // BLOCK
    bufs = (buf0, buf1, buf2, buf3)

    state[:, HALO : HALO + own] = done[...]
    edge = jnp.zeros((224, REACH), jnp.bfloat16)
    buf0[:, 0:REACH] = edge
    buf0[:, REACH + wide : REACH + wide + REACH] = edge
    buf2[:, 2 * REACH : 3 * REACH] = edge
    buf2[:, wide - REACH : wide] = edge

    def carry_over(step, first, last):
        source, target = (own0, own1, own2, own3)[step % 4], bufs[step % 4]
        for low, high in ((first, last), (own - last, own - first)):
            target[:, REACH + HALO + low : REACH + HALO + high] = source[:, low:high]

    for step in range(STEPS - 1):
        inside = interior_blocks(step, own // BLOCK)
        if step % 2 == 0:
            carry_over(step, inside[0] * BLOCK, min(inside[0] * BLOCK + BLOCK + REACH, own // 2))
        else:
            carry_over(step, inside[0] * BLOCK, inside[0] * BLOCK + REACH)

    for which, part in ((0, left), (1, right)):
        for index in range(fringe):
            block = which * fringe + index
            value = part[:, index * BLOCK : (index + 1) * BLOCK]
            coeff = 0.5 * value[63:64]
            here = which * (HALO + own) + index * BLOCK
            state[0:56, here : here + BLOCK] = value[0:56]
            state[56:64, here : here + BLOCK] = jnp.broadcast_to(coeff, (8, BLOCK))
            store_parts(buf0, here + REACH, split(value[0:56], coeff))

            def store(down, across, piece):
                outer[block, down * LANES : (down + 1) * LANES, across * LANES : (across + 1) * LANES] = piece

            build_block(value[56:63], store)

    def adjacency(block):
        if block < fringe:
            return outer[block]
        if block < blocks - fringe:
            return inner[block - fringe]
        return outer[block - (blocks - 2 * fringe)]

    for step in range(1, STEPS + 1):
        inside = [fringe + block for block in interior_blocks(step, own // BLOCK)]
        places = [
            (block * BLOCK, BLOCK, functools.partial(adjacency, block), True)
            for block in range(step // 2, blocks - step // 2)
            if block not in inside
        ]
        sweep(state, bufs[(step - 1) % 4], bufs[step % 4] if step < STEPS else None, REACH, places)

    square[...] = jnp.zeros(square.shape, jnp.float32)
    square[0:LEVELS, 0:LEVELS] = root[...]
    matrix = lax.dot_general(
        square[...], square[...], (((1,), (1,)), ((), ())),
        precision=lax.Precision.HIGHEST, preferred_element_type=jnp.float32,
    )
    matrix_high = matrix.astype(jnp.bfloat16)
    matrix_low = (matrix - matrix_high.astype(jnp.float32)).astype(jnp.bfloat16)
    stacked = jnp.concatenate([matrix_high, matrix_low], axis=0)
    total = jnp.zeros((1, BLOCK), jnp.float32)
    for block in range(own // BLOCK):
        value = state[:, HALO + block * BLOCK : HALO + (block + 1) * BLOCK]
        high = value.astype(jnp.bfloat16)
        low = (value - high.astype(jnp.float32)).astype(jnp.bfloat16)
        first = jnp.dot(stacked, high, preferred_element_type=jnp.float32)
        second = jnp.dot(matrix_high, low, preferred_element_type=jnp.float32)
        smoothed = first[0:LEVELS] + (first[64 : 64 + LEVELS] + second[0:LEVELS])
        source = head if block < own // BLOCK // 2 else tail
        at = (block * BLOCK) % head.shape[1]
        total = total + jnp.sum(source[0:LEVELS, at : at + BLOCK] * smoothed, axis=0, keepdims=True)
        for tile in range(BLOCK // LANES):
            spot = block * (BLOCK // LANES) + tile
            rowed[pl.ds(spot, LEVELS, stride=tiles), :] = smoothed[:, tile * LANES : (tile + 1) * LANES]
    slots = 4
    chunk = rowed.shape[0] // slots
    spot = pl.ds(slots * chunk, 8)
    keep[spot, :] = send[spot, :] = jnp.broadcast_to(jnp.sum(total, axis=1, keepdims=True), (8, LANES))

    mine, chip = ids[0], ids[1]
    spare = slots * chunk - LEVELS * tiles

    def products(slot, start, first, count):
        rows = rowed[pl.ds(pl.multiple_of(start + first, 8), count), :]
        at = 2 * (start + first)
        here = pl.ds(slot * chunk + first, count)
        keep[here, :] = ens[pl.ds(at + mine, count, stride=2), :] * rows
        send[here, :] = ens[pl.ds(at + 1 - mine, count, stride=2), :] * rows

    for slot in range(slots):
        target = lax.rem(chip + slot, slots)
        start = target * chunk
        products(slot, start, 0, chunk - spare)

        @pl.when(target < slots - 1)
        def _():
            products(slot, start, chunk - spare, spare)

        @pl.when(target == slots - 1)
        def _():
            nothing = jnp.zeros((spare, LANES), jnp.float32)
            keep[pl.ds((slot + 1) * chunk - spare, spare), :] = nothing
            send[pl.ds((slot + 1) * chunk - spare, spare), :] = nothing


def place_kernel(scale, ids, same, other, out, quadratic, lines, sems):
    mine, chip = ids[0], ids[1]
    slots = same.shape[0]
    chunk = lines.shape[0] // slots // 2
    short = 2 * chunk - (lines.shape[0] - out.shape[0])

    def copies(slot):
        source = lax.rem(chip + slots - slot, slots)
        start = pl.multiple_of(source * 2 * chunk, 8)
        rows = pl.ds(start, short)
        rest = pl.ds(pl.multiple_of(start + short, 8), 2 * chunk - short)
        return source, start, (
            pltpu.make_async_copy(lines.at[rows], out.at[rows], sems.at[0, slot]),
            pltpu.make_async_copy(lines.at[rest], out.at[rest], sems.at[1, slot]),
        )

    for slot in range(slots):
        source, start, (main, extra) = copies(slot)
        lines[pl.ds(start + mine, chunk, stride=2), :] = same[slot, 0:chunk, :]
        lines[pl.ds(start + 1 - mine, chunk, stride=2), :] = other[slot, 0:chunk, :]
        main.start()
        pl.when(source < slots - 1)(extra.start)
    terms = [same[slot, chunk : chunk + 8, :] for slot in range(slots)]
    quadratic[0, 0] = jnp.max((terms[0] + terms[2]) + (terms[1] + terms[3])) * scale
    for slot in range(slots):
        source, start, (main, extra) = copies(slot)
        main.wait()
        pl.when(source < slots - 1)(extra.wait)


def interleave(array):
    cells = array.shape[2]
    array = array.reshape(2, LEVELS, cells // LANES, LANES)
    return array.transpose(1, 2, 0, 3).reshape(-1, LANES)


def on_device(ensemble, field, diffusivity, neighbours, vertical_root):
    own = diffusivity.shape[0]
    patches = lax.axis_size("patch")
    members = lax.axis_size("mem")
    chips = members // 2
    all_cells = own * patches
    half = own // 2
    tiles = own // LANES
    vmem = pl.BlockSpec(memory_space=pltpu.VMEM)
    smem = pl.BlockSpec(memory_space=pltpu.SMEM)
    hbm = pl.BlockSpec(memory_space=pltpu.HBM)
    params = pltpu.CompilerParams(vmem_limit_bytes=32 * 1024 * 1024)
    place = (lax.axis_index("patch") * own).astype(jnp.int32).reshape(1)
    member = lax.axis_index("mem")
    ids = jnp.stack([lax.rem(member, 2), member // 2]).astype(jnp.int32)
    ens_rows = interleave(ensemble[0])
    field_rows = interleave(field)

    in_hbm = [
        pltpu.with_memory_space_constraint(array, pltpu.HBM)
        for array in (ens_rows, field_rows, diffusivity.reshape(1, own), neighbours)
    ]
    side = jax.ShapeDtypeStruct((64, half), jnp.float32)
    head, tail = pl.pallas_call(
        functools.partial(prepare_kernel, all_cells),
        out_shape=(side, side),
        in_specs=[smem, hbm, hbm, hbm, hbm],
        out_specs=(vmem, vmem),
        scratch_shapes=[
            pltpu.VMEM(ens_rows.shape, jnp.float32),
            pltpu.VMEM(ens_rows.shape, jnp.float32),
            pltpu.VMEM((1, own), jnp.float32),
            pltpu.VMEM((7, own), jnp.int32),
            pltpu.SemaphoreType.DMA((3, 4)),
        ],
        compiler_params=params,
        name="prepare",
    )(place, *in_hbm)

    left = lax.ppermute(tail, "patch", [(i, (i + 1) % patches) for i in range(patches)])
    right = lax.ppermute(head, "patch", [((i + 1) % patches, i) for i in range(patches)])

    parts = jax.ShapeDtypeStruct((224, own), jnp.bfloat16)
    inside = pl.pallas_call(
        interior_kernel,
        out_shape=(
            jax.ShapeDtypeStruct((own // BLOCK, 2 * BLOCK, BLOCK), jnp.bfloat16),
            jax.ShapeDtypeStruct((64, own), jnp.float32),
            parts, parts, parts, parts,
        ),
        in_specs=[vmem] * 2,
        out_specs=(vmem,) * 6,
        compiler_params=params,
        cost_estimate=pl.CostEstimate(flops=4_000_000_000, bytes_accessed=4_000_000, transcendentals=0),
        name="interior",
    )(head, tail)

    wide = own + 2 * HALO
    chunk = 56 * tiles // chips
    terms = jax.ShapeDtypeStruct((chips * chunk + 8, LANES), jnp.float32)
    wide_parts = pltpu.VMEM((224, wide + 2 * REACH), jnp.bfloat16)
    keep, send = pl.pallas_call(
        smooth_kernel,
        out_shape=(terms, terms),
        in_specs=[smem] + [vmem] * 12,
        out_specs=(vmem, vmem),
        scratch_shapes=[
            pltpu.VMEM((64, wide), jnp.float32),
            pltpu.VMEM((2 * HALO // BLOCK, 2 * BLOCK, BLOCK), jnp.bfloat16),
            wide_parts, wide_parts, wide_parts, wide_parts,
            pltpu.VMEM((64, 64), jnp.float32),
            pltpu.VMEM((56 * tiles, LANES), jnp.float32),
        ],
        compiler_params=params,
        name="smooth",
    )(ids, left, head, tail, right, vertical_root, ens_rows, *inside)

    def shift_chips(array, by):
        pairs = [(2 * z + c, 2 * ((z + by) % chips) + c) for z in range(chips) for c in range(2)]
        return lax.ppermute(array, "mem", pairs)

    twin = [(i, i ^ 1) for i in range(members)]
    order = [2, 1, 3]
    pair_sum = keep + lax.ppermute(send, "mem", twin)
    pieces = [pair_sum[chunk * slot : chunk * (slot + 1)] for slot in range(chips)]
    terms = {by: shift_chips(pieces[by], by) for by in order}
    spread = jnp.broadcast_to(pair_sum[chips * chunk : chips * chunk + 1][None], (patches, 1, LANES))
    spread = lax.all_to_all(spread, "patch", 0, 0)
    terms, spread = lax.optimization_barrier((terms, spread))
    total = (pieces[0] + terms[1] + terms[2] + terms[3]) / (members - 1.0)
    total = jnp.concatenate([total, jnp.broadcast_to(jnp.sum(spread, axis=0), (8, LANES))], axis=0)
    copies = {by: shift_chips(total, by) for by in order}
    same = jnp.stack([total, copies[1], copies[2], copies[3]])
    other = lax.ppermute(same, "mem", twin)
    scale = 1.0 / ((members - 1.0) * field.shape[0] * field.shape[1] * all_cells)
    rows, quadratic = pl.pallas_call(
        functools.partial(place_kernel, scale),
        out_shape=(
            jax.ShapeDtypeStruct(field_rows.shape, jnp.float32),
            jax.ShapeDtypeStruct((1, 1), jnp.float32),
        ),
        in_specs=[smem, vmem, vmem],
        out_specs=(hbm, smem),
        scratch_shapes=[
            pltpu.VMEM((chips * chunk * 2, LANES), jnp.float32),
            pltpu.SemaphoreType.DMA((2, chips)),
        ],
        compiler_params=params,
        name="place",
    )(ids, same, other)
    product = rows.reshape(LEVELS, tiles, 2, LANES).transpose(2, 0, 1, 3).reshape(field.shape)
    return (product, quadratic.reshape(()))


def solution(mesh):
    return jax.shard_map(
        on_device,
        mesh=mesh,
        in_specs=(
            P("mem", None, None, "patch"),
            P(None, None, "patch"),
            P("patch"),
            P(None, "patch"),
            P(),
        ),
        out_specs=(P(None, None, "patch"), P()),
        check_vma=False,
    )
```

```python
import functools

import jax
import jax.numpy as jnp
from jax import lax
from jax.experimental import pallas as pl
from jax.experimental.pallas import tpu as pltpu
from jax.sharding import PartitionSpec as P

STEPS = 8
REACH = 128
BLOCK = 256
HALO = STEPS * REACH
LEVELS = 55
LANES = 128


def prepare_kernel(
    all_cells, place, ens, field, diff, neigh, head, tail, ens_in, field_in, diff_in, neigh_in, sems
):
    own = diff.shape[1]
    tiles = own // LANES
    half = own // 2
    start = place[0]
    levels = (0, 16, 32, 48, LEVELS)
    copies = []
    for turn in range(4):
        rows = pl.ds(levels[turn] * 2 * tiles, (levels[turn + 1] - levels[turn]) * 2 * tiles)
        copies.append((
            pltpu.make_async_copy(ens.at[rows], ens_in.at[rows], sems.at[0, turn]),
            pltpu.make_async_copy(field.at[rows], field_in.at[rows], sems.at[1, turn]),
        ))
    others = (
        pltpu.make_async_copy(neigh, neigh_in, sems.at[2, 0]),
        pltpu.make_async_copy(diff, diff_in, sems.at[2, 1]),
    )
    for copy in others + copies[0] + copies[1] + copies[2] + copies[3]:
        copy.start()
    for copy in others:
        copy.wait()
    for part, out in ((0, head), (1, tail)):
        cols = pl.ds(part * half, half)
        out[55:56, :] = jnp.ones((1, half), jnp.float32)
        cell = lax.broadcasted_iota(jnp.int32, (7, half), 1) + (start + part * half)
        shift = neigh_in[:, cols] - cell
        shift = jnp.where(shift > all_cells // 2, shift - all_cells, shift)
        shift = jnp.where(shift < -(all_cells // 2), shift + all_cells, shift)
        out[56:63, :] = shift.astype(jnp.float32)
        out[63:64, :] = diff_in[:, cols]
    for turn in range(4):
        for copy in copies[turn]:
            copy.wait()
        low, high = levels[turn], levels[turn + 1]
        rows = pl.ds(low * 2 * tiles, (high - low) * 2 * tiles)
        ens_in[rows, :] = ens_in[rows, :] * field_in[rows, :]
        for part, out in ((0, head), (1, tail)):
            for tile in range(tiles // 2):
                at = low * 2 * tiles + 2 * (part * (tiles // 2) + tile)
                out[low:high, tile * LANES : (tile + 1) * LANES] = (
                    ens_in[pl.ds(at, high - low, stride=2 * tiles), :]
                    + ens_in[pl.ds(at + 1, high - low, stride=2 * tiles), :]
                )


def build_block(shift, store):
    row = lax.broadcasted_iota(jnp.int32, (LANES, LANES), 0).astype(jnp.float32).astype(jnp.bfloat16)
    lane = lax.broadcasted_iota(jnp.int32, (1, LANES), 1).astype(jnp.float32)
    one = jnp.ones((LANES, LANES), jnp.bfloat16)
    zero = jnp.zeros((LANES, LANES), jnp.bfloat16)
    for chunk in range(BLOCK // LANES):
        part = shift[:, chunk * LANES : (chunk + 1) * LANES]
        for side in range(3):
            local = part + (lane + (1.0 - side) * LANES)
            inside = jnp.logical_and(jnp.logical_and(local >= 0.0, local < LANES), part != 0.0)
            local = jnp.where(inside, local, -1.0).astype(jnp.bfloat16)
            hit = zero
            for slot in range(7):
                hit = jnp.where(row == local[slot : slot + 1, :], one, hit)
            store(chunk + side, chunk, hit)
        store((chunk + 3) % 4, chunk, zero)


def split(value, coeff):
    both = jnp.concatenate([value, coeff * value], axis=0)
    high = both.astype(jnp.bfloat16)
    low = (both - high.astype(jnp.float32)).astype(jnp.bfloat16)
    return high, low


def store_parts(buf, at, parts):
    width = parts[0].shape[1]
    buf[0:112, at : at + width] = parts[0]
    buf[112:224, at : at + width] = parts[1]


def sweep(state, now, later, margin, places):
    def matmul(at, width, matrix):
        window = now[:, at + margin - REACH : at + margin + width + REACH]
        return jnp.dot(window, matrix, preferred_element_type=jnp.float32)

    def finish(at, width, kept, total):
        coeff = state[56:57, at : at + width]
        value = state[0:56, at : at + width]
        change = coeff * (total[0:56] + total[112:168]) + (total[56:112] + total[168:224])
        value = value * (1.0 - change[55:56]) + change
        if kept:
            state[0:56, at : at + width] = value
        if later is not None:
            store_parts(later, at + margin, split(value, coeff))

    waiting = None
    for at, width, matrix, kept in places:
        total = matmul(at, width, matrix())
        if waiting is not None:
            finish(*waiting)
        waiting = (at, width, kept, total)
    finish(*waiting)


def interior_blocks(step, count):
    skip = (step + 1) // 2
    return range(skip, count - skip)


def interior_kernel(head, tail, adj, state, buf0, buf1, buf2, buf3):
    bufs = (buf0, buf1, buf2, buf3)
    blocks = adj.shape[0]
    half = blocks // 2
    for block in range(blocks):
        source, at = (head, block * BLOCK) if block < half else (tail, (block - half) * BLOCK)

        def store(down, across, value):
            adj[block, down * LANES : (down + 1) * LANES, across * LANES : (across + 1) * LANES] = value

        value = source[:, at : at + BLOCK]
        build_block(value[56:63], store)
        coeff = 0.5 * value[63:64]
        here = block * BLOCK
        state[0:56, here : here + BLOCK] = value[0:56]
        state[56:64, here : here + BLOCK] = jnp.broadcast_to(coeff, (8, BLOCK))
        store_parts(buf0, here, split(value[0:56], coeff))
    for step in range(1, STEPS - 1):
        whole = interior_blocks(step, blocks)
        places = [(block * BLOCK, BLOCK, functools.partial(lambda b: adj[b], block), True) for block in whole]
        if step % 2:
            low, high = whole[0] - 1, whole[-1] + 1
            places.append((low * BLOCK + REACH, REACH, lambda: adj[low, REACH:, REACH:], False))
            places.append((high * BLOCK, REACH, lambda: adj[high, : BLOCK + REACH, :REACH], False))
        sweep(state, bufs[(step - 1) % 4], bufs[step % 4], 0, places)


def smooth_kernel(
    ids, left, head, tail, right, root, ens, inner, done, own0, own1, own2, own3,
    keep, send, state, outer, buf0, buf1, buf2, buf3, square, rowed,
):
    wide = state.shape[1]
    own = wide - 2 * HALO
    tiles = own // LANES
    blocks = wide // BLOCK
    fringe = HALO // BLOCK
    bufs = (buf0, buf1, buf2, buf3)

    state[:, HALO : HALO + own] = done[...]
    edge = jnp.zeros((224, REACH), jnp.bfloat16)
    buf0[:, 0:REACH] = edge
    buf0[:, REACH + wide : REACH + wide + REACH] = edge
    buf2[:, 2 * REACH : 3 * REACH] = edge
    buf2[:, wide - REACH : wide] = edge

    def carry_over(step, first, last):
        source, target = (own0, own1, own2, own3)[step % 4], bufs[step % 4]
        for low, high in ((first, last), (own - last, own - first)):
            target[:, REACH + HALO + low : REACH + HALO + high] = source[:, low:high]

    for step in range(STEPS - 1):
        inside = interior_blocks(step, own // BLOCK)
        if step % 2 == 0:
            carry_over(step, inside[0] * BLOCK, min(inside[0] * BLOCK + BLOCK + REACH, own // 2))
        else:
            carry_over(step, inside[0] * BLOCK, inside[0] * BLOCK + REACH)

    for which, part in ((0, left), (1, right)):
        for index in range(fringe):
            block = which * fringe + index
            value = part[:, index * BLOCK : (index + 1) * BLOCK]
            coeff = 0.5 * value[63:64]
            here = which * (HALO + own) + index * BLOCK
            state[0:56, here : here + BLOCK] = value[0:56]
            state[56:64, here : here + BLOCK] = jnp.broadcast_to(coeff, (8, BLOCK))
            store_parts(buf0, here + REACH, split(value[0:56], coeff))

            def store(down, across, piece):
                outer[block, down * LANES : (down + 1) * LANES, across * LANES : (across + 1) * LANES] = piece

            build_block(value[56:63], store)

    def adjacency(block):
        if block < fringe:
            return outer[block]
        if block < blocks - fringe:
            return inner[block - fringe]
        return outer[block - (blocks - 2 * fringe)]

    for step in range(1, STEPS + 1):
        inside = [fringe + block for block in interior_blocks(step, own // BLOCK)]
        places = [
            (block * BLOCK, BLOCK, functools.partial(adjacency, block), True)
            for block in range(step // 2, blocks - step // 2)
            if block not in inside
        ]
        sweep(state, bufs[(step - 1) % 4], bufs[step % 4] if step < STEPS else None, REACH, places)

    square[...] = jnp.zeros(square.shape, jnp.float32)
    square[0:LEVELS, 0:LEVELS] = root[...]
    matrix = lax.dot_general(
        square[...], square[...], (((1,), (1,)), ((), ())),
        precision=lax.Precision.HIGHEST, preferred_element_type=jnp.float32,
    )
    matrix_high = matrix.astype(jnp.bfloat16)
    matrix_low = (matrix - matrix_high.astype(jnp.float32)).astype(jnp.bfloat16)
    stacked = jnp.concatenate([matrix_high, matrix_low], axis=0)
    total = jnp.zeros((1, BLOCK), jnp.float32)
    for block in range(own // BLOCK):
        value = state[:, HALO + block * BLOCK : HALO + (block + 1) * BLOCK]
        high = value.astype(jnp.bfloat16)
        low = (value - high.astype(jnp.float32)).astype(jnp.bfloat16)
        first = jnp.dot(stacked, high, preferred_element_type=jnp.float32)
        second = jnp.dot(matrix_high, low, preferred_element_type=jnp.float32)
        smoothed = first[0:LEVELS] + (first[64 : 64 + LEVELS] + second[0:LEVELS])
        source = head if block < own // BLOCK // 2 else tail
        at = (block * BLOCK) % head.shape[1]
        total = total + jnp.sum(source[0:LEVELS, at : at + BLOCK] * smoothed, axis=0, keepdims=True)
        for tile in range(BLOCK // LANES):
            spot = block * (BLOCK // LANES) + tile
            rowed[pl.ds(spot, LEVELS, stride=tiles), :] = smoothed[:, tile * LANES : (tile + 1) * LANES]
    slots = 4
    chunk = rowed.shape[0] // slots
    pitch = chunk + 8
    spare_rows = jnp.broadcast_to(jnp.sum(total, axis=1, keepdims=True), (8, LANES))
    mine, chip = ids[0], ids[1]
    spare = slots * chunk - LEVELS * tiles

    def products(slot, start, first, count):
        rows = rowed[pl.ds(pl.multiple_of(start + first, 8), count), :]
        at = 2 * (start + first)
        here = pl.ds(slot * pitch + first, count)
        keep[here, :] = ens[pl.ds(at + mine, count, stride=2), :] * rows
        send[here, :] = ens[pl.ds(at + 1 - mine, count, stride=2), :] * rows

    for slot in range(slots):
        target = lax.rem(chip + slot, slots)
        start = target * chunk
        keep[pl.ds(slot * pitch + chunk, 8), :] = spare_rows
        send[pl.ds(slot * pitch + chunk, 8), :] = spare_rows
        products(slot, start, 0, chunk - spare)

        @pl.when(target < slots - 1)
        def _():
            products(slot, start, chunk - spare, spare)

        @pl.when(target == slots - 1)
        def _():
            nothing = jnp.zeros((spare, LANES), jnp.float32)
            keep[pl.ds(slot * pitch + chunk - spare, spare), :] = nothing
            send[pl.ds(slot * pitch + chunk - spare, spare), :] = nothing


def place_kernel(scale, ids, same, other, spread, out, quadratic, lines, sems):
    mine, chip = ids[0], ids[1]
    slots = same.shape[0]
    chunk = lines.shape[0] // slots // 2
    short = 2 * chunk - (lines.shape[0] - out.shape[0])

    def copies(slot):
        source = lax.rem(chip + slots - slot, slots)
        start = pl.multiple_of(source * 2 * chunk, 8)
        rows = pl.ds(start, short)
        rest = pl.ds(pl.multiple_of(start + short, 8), 2 * chunk - short)
        return source, start, (
            pltpu.make_async_copy(lines.at[rows], out.at[rows], sems.at[0, slot]),
            pltpu.make_async_copy(lines.at[rest], out.at[rest], sems.at[1, slot]),
        )

    for slot in range(slots):
        source, start, (main, extra) = copies(slot)
        lines[pl.ds(start + mine, chunk, stride=2), :] = same[slot, 0:chunk, :]
        lines[pl.ds(start + 1 - mine, chunk, stride=2), :] = other[slot, 0:chunk, :]
        main.start()
        pl.when(source < slots - 1)(extra.start)
    quadratic[0, 0] = jnp.max(jnp.sum(spread[...], axis=0, keepdims=True)) * scale
    for slot in range(slots):
        source, start, (main, extra) = copies(slot)
        main.wait()
        pl.when(source < slots - 1)(extra.wait)


def interleave(array):
    cells = array.shape[2]
    array = array.reshape(2, LEVELS, cells // LANES, LANES)
    return array.transpose(1, 2, 0, 3).reshape(-1, LANES)


def on_device(ensemble, field, diffusivity, neighbours, vertical_root):
    own = diffusivity.shape[0]
    patches = lax.axis_size("patch")
    members = lax.axis_size("mem")
    chips = members // 2
    all_cells = own * patches
    half = own // 2
    tiles = own // LANES
    vmem = pl.BlockSpec(memory_space=pltpu.VMEM)
    smem = pl.BlockSpec(memory_space=pltpu.SMEM)
    hbm = pl.BlockSpec(memory_space=pltpu.HBM)
    params = pltpu.CompilerParams(vmem_limit_bytes=32 * 1024 * 1024)
    place = (lax.axis_index("patch") * own).astype(jnp.int32).reshape(1)
    member = lax.axis_index("mem")
    ids = jnp.stack([lax.rem(member, 2), member // 2]).astype(jnp.int32)
    ens_rows = interleave(ensemble[0])
    field_rows = interleave(field)

    in_hbm = [
        pltpu.with_memory_space_constraint(array, pltpu.HBM)
        for array in (ens_rows, field_rows, diffusivity.reshape(1, own), neighbours)
    ]
    side = jax.ShapeDtypeStruct((64, half), jnp.float32)
    head, tail = pl.pallas_call(
        functools.partial(prepare_kernel, all_cells),
        out_shape=(side, side),
        in_specs=[smem, hbm, hbm, hbm, hbm],
        out_specs=(vmem, vmem),
        scratch_shapes=[
            pltpu.VMEM(ens_rows.shape, jnp.float32),
            pltpu.VMEM(ens_rows.shape, jnp.float32),
            pltpu.VMEM((1, own), jnp.float32),
            pltpu.VMEM((7, own), jnp.int32),
            pltpu.SemaphoreType.DMA((3, 4)),
        ],
        compiler_params=params,
        name="prepare",
    )(place, *in_hbm)

    odd = lax.rem(lax.axis_index("patch"), 2) == 1
    first = jnp.where(odd, tail, head)
    second = jnp.where(odd, head, tail)
    swaps = [[], []]
    for low in range(patches):
        high = (low + 1) % patches
        swaps[low % 2] += [(low, high), (high, low)]
    first = lax.ppermute(first, "patch", swaps[1])
    second = lax.ppermute(second, "patch", swaps[0])
    left = jnp.where(odd, second, first)
    right = jnp.where(odd, first, second)

    parts = jax.ShapeDtypeStruct((224, own), jnp.bfloat16)
    inside = pl.pallas_call(
        interior_kernel,
        out_shape=(
            jax.ShapeDtypeStruct((own // BLOCK, 2 * BLOCK, BLOCK), jnp.bfloat16),
            jax.ShapeDtypeStruct((64, own), jnp.float32),
            parts, parts, parts, parts,
        ),
        in_specs=[vmem] * 2,
        out_specs=(vmem,) * 6,
        compiler_params=params,
        cost_estimate=pl.CostEstimate(flops=4_000_000_000, bytes_accessed=4_000_000, transcendentals=0),
        name="interior",
    )(head, tail)

    wide = own + 2 * HALO
    chunk = 56 * tiles // chips
    terms = jax.ShapeDtypeStruct((chips * (chunk + 8), LANES), jnp.float32)
    wide_parts = pltpu.VMEM((224, wide + 2 * REACH), jnp.bfloat16)
    keep, send = pl.pallas_call(
        smooth_kernel,
        out_shape=(terms, terms),
        in_specs=[smem] + [vmem] * 12,
        out_specs=(vmem, vmem),
        scratch_shapes=[
            pltpu.VMEM((64, wide), jnp.float32),
            pltpu.VMEM((2 * HALO // BLOCK, 2 * BLOCK, BLOCK), jnp.bfloat16),
            wide_parts, wide_parts, wide_parts, wide_parts,
            pltpu.VMEM((64, 64), jnp.float32),
            pltpu.VMEM((56 * tiles, LANES), jnp.float32),
        ],
        compiler_params=params,
        name="smooth",
    )(ids, left, head, tail, right, vertical_root, ens_rows, *inside)

    def shift_chips(array, by):
        pairs = [(2 * z + c, 2 * ((z + by) % chips) + c) for z in range(chips) for c in range(2)]
        return lax.ppermute(array, "mem", pairs)

    twin = [(i, i ^ 1) for i in range(members)]
    order = [2, 1, 3]
    pair_sum = keep + lax.ppermute(send, "mem", twin)
    pitch = chunk + 8
    pieces = [pair_sum[pitch * slot : pitch * (slot + 1)] for slot in range(chips)]
    terms = {by: shift_chips(pieces[by], by) for by in order}
    total = ((terms[3] + terms[1]) + (terms[2] + pieces[0])) / (members - 1.0)
    mine = total[0:chunk]
    copies = {by: shift_chips(mine, by) for by in order}
    spread = jnp.broadcast_to(total[chunk : chunk + 1][None], (patches, 1, LANES))
    spread = lax.all_to_all(spread, "patch", 0, 0)
    copies, spread = lax.optimization_barrier((copies, spread))
    same = jnp.stack([mine, copies[1], copies[2], copies[3]])
    other = lax.ppermute(same, "mem", twin)
    scale = 1.0 / (field.shape[0] * field.shape[1] * all_cells)
    rows, quadratic = pl.pallas_call(
        functools.partial(place_kernel, scale),
        out_shape=(
            jax.ShapeDtypeStruct(field_rows.shape, jnp.float32),
            jax.ShapeDtypeStruct((1, 1), jnp.float32),
        ),
        in_specs=[smem, vmem, vmem, vmem],
        out_specs=(hbm, smem),
        scratch_shapes=[
            pltpu.VMEM((chips * chunk * 2, LANES), jnp.float32),
            pltpu.SemaphoreType.DMA((2, chips)),
        ],
        compiler_params=params,
        name="place",
    )(ids, same, other, spread.reshape(patches, LANES))
    product = rows.reshape(LEVELS, tiles, 2, LANES).transpose(2, 0, 1, 3).reshape(field.shape)
    return (product, quadratic.reshape(()))


def solution(mesh):
    return jax.shard_map(
        on_device,
        mesh=mesh,
        in_specs=(
            P("mem", None, None, "patch"),
            P(None, None, "patch"),
            P("patch"),
            P(None, "patch"),
            P(),
        ),
        out_specs=(P(None, None, "patch"), P()),
        check_vma=False,
    )
```

```python
import functools

import jax
import jax.numpy as jnp
from jax import lax
from jax.experimental import pallas as pl
from jax.experimental.pallas import tpu as pltpu
from jax.sharding import PartitionSpec as P

STEPS = 8
REACH = 128
BLOCK = 256
HALO = STEPS * REACH
LEVELS = 55
LANES = 128
EARLY, LATE = (0, 2), (1, 3)


def prepare_kernel(
    all_cells, place, ens, field, diff, neigh, head, tail, ens_in, field_in, diff_in, neigh_in, sems
):
    own = diff.shape[1]
    tiles = own // LANES
    half = own // 2
    start = place[0]
    levels = (0, 16, 32, 48, LEVELS)
    copies = []
    for turn in range(4):
        rows = pl.ds(levels[turn] * 2 * tiles, (levels[turn + 1] - levels[turn]) * 2 * tiles)
        copies.append((
            pltpu.make_async_copy(ens.at[rows], ens_in.at[rows], sems.at[0, turn]),
            pltpu.make_async_copy(field.at[rows], field_in.at[rows], sems.at[1, turn]),
        ))
    others = (
        pltpu.make_async_copy(neigh, neigh_in, sems.at[2, 0]),
        pltpu.make_async_copy(diff, diff_in, sems.at[2, 1]),
    )
    for copy in others + copies[0] + copies[1] + copies[2] + copies[3]:
        copy.start()
    for copy in others:
        copy.wait()
    for part, out in ((0, head), (1, tail)):
        cols = pl.ds(part * half, half)
        out[55:56, :] = jnp.ones((1, half), jnp.float32)
        cell = lax.broadcasted_iota(jnp.int32, (7, half), 1) + (start + part * half)
        shift = neigh_in[:, cols] - cell
        shift = jnp.where(shift > all_cells // 2, shift - all_cells, shift)
        shift = jnp.where(shift < -(all_cells // 2), shift + all_cells, shift)
        out[56:63, :] = shift.astype(jnp.float32)
        out[63:64, :] = diff_in[:, cols]
    for turn in range(4):
        for copy in copies[turn]:
            copy.wait()
        low, high = levels[turn], levels[turn + 1]
        rows = pl.ds(low * 2 * tiles, (high - low) * 2 * tiles)
        ens_in[rows, :] = ens_in[rows, :] * field_in[rows, :]
        for part, out in ((0, head), (1, tail)):
            for tile in range(tiles // 2):
                at = low * 2 * tiles + 2 * (part * (tiles // 2) + tile)
                out[low:high, tile * LANES : (tile + 1) * LANES] = (
                    ens_in[pl.ds(at, high - low, stride=2 * tiles), :]
                    + ens_in[pl.ds(at + 1, high - low, stride=2 * tiles), :]
                )


def build_block(shift, store):
    row = lax.broadcasted_iota(jnp.int32, (LANES, LANES), 0).astype(jnp.float32).astype(jnp.bfloat16)
    lane = lax.broadcasted_iota(jnp.int32, (1, LANES), 1).astype(jnp.float32)
    one = jnp.ones((LANES, LANES), jnp.bfloat16)
    zero = jnp.zeros((LANES, LANES), jnp.bfloat16)
    for chunk in range(BLOCK // LANES):
        part = shift[:, chunk * LANES : (chunk + 1) * LANES]
        for side in range(3):
            local = part + (lane + (1.0 - side) * LANES)
            inside = jnp.logical_and(jnp.logical_and(local >= 0.0, local < LANES), part != 0.0)
            local = jnp.where(inside, local, -1.0).astype(jnp.bfloat16)
            hit = zero
            for slot in range(7):
                hit = jnp.where(row == local[slot : slot + 1, :], one, hit)
            store(chunk + side, chunk, hit)
        store((chunk + 3) % 4, chunk, zero)


def split(value, coeff):
    both = jnp.concatenate([value, coeff * value], axis=0)
    high = both.astype(jnp.bfloat16)
    low = (both - high.astype(jnp.float32)).astype(jnp.bfloat16)
    return high, low


def store_parts(buf, at, parts):
    width = parts[0].shape[1]
    buf[0:112, at : at + width] = parts[0]
    buf[112:224, at : at + width] = parts[1]


def sweep(state, now, later, bases, places):
    first, origin = bases

    def matmul(at, width, matrix):
        low = at - origin - REACH
        return jnp.dot(now[:, low : low + width + 2 * REACH], matrix, preferred_element_type=jnp.float32)

    def finish(at, width, kept, total):
        here = slice(at - first, at - first + width)
        coeff = state[56:57, here]
        value = state[0:56, here]
        change = coeff * (total[0:56] + total[112:168]) + (total[56:112] + total[168:224])
        value = value * (1.0 - change[55:56]) + change
        if kept:
            state[0:56, here] = value
        if later is not None:
            store_parts(later, at - origin, split(value, coeff))

    waiting = None
    for at, width, matrix, kept in places:
        total = matmul(at, width, matrix())
        if waiting is not None:
            finish(*waiting)
        waiting = (at, width, kept, total)
    finish(*waiting)


def interior_blocks(step, count):
    skip = (step + 1) // 2
    return range(skip, count - skip)


def interior_kernel(head, tail, adj, state, buf0, buf1, buf2, buf3):
    bufs = (buf0, buf1, buf2, buf3)
    blocks = adj.shape[0]
    half = blocks // 2
    for block in range(blocks):
        source, at = (head, block * BLOCK) if block < half else (tail, (block - half) * BLOCK)

        def store(down, across, value):
            adj[block, down * LANES : (down + 1) * LANES, across * LANES : (across + 1) * LANES] = value

        value = source[:, at : at + BLOCK]
        build_block(value[56:63], store)
        coeff = 0.5 * value[63:64]
        here = block * BLOCK
        state[0:56, here : here + BLOCK] = value[0:56]
        state[56:64, here : here + BLOCK] = jnp.broadcast_to(coeff, (8, BLOCK))
        store_parts(buf0, here, split(value[0:56], coeff))
    for step in range(1, STEPS - 1):
        whole = interior_blocks(step, blocks)
        places = [(block * BLOCK, BLOCK, functools.partial(lambda b: adj[b], block), True) for block in whole]
        if step % 2:
            low, high = whole[0] - 1, whole[-1] + 1
            places.append((low * BLOCK + REACH, REACH, lambda: adj[low, REACH:, REACH:], False))
            places.append((high * BLOCK, REACH, lambda: adj[high, : BLOCK + REACH, :REACH], False))
        sweep(state, bufs[(step - 1) % 4], bufs[step % 4], (0, 0), places)


def load_halo(part, at, state, outer, buf, bases):
    for index in range(HALO // BLOCK):
        value = part[:, index * BLOCK : (index + 1) * BLOCK]
        coeff = 0.5 * value[63:64]
        here = at + index * BLOCK
        spot = slice(here - bases[0], here - bases[0] + BLOCK)
        state[0:56, spot] = value[0:56]
        state[56:64, spot] = jnp.broadcast_to(coeff, (8, BLOCK))
        store_parts(buf, here - bases[1], split(value[0:56], coeff))

        def store(down, across, piece):
            outer[index, down * LANES : (down + 1) * LANES, across * LANES : (across + 1) * LANES] = piece

        build_block(value[56:63], store)


def carry_over(owns, bufs, side, bases):
    own = owns[0].shape[1]
    for step in range(STEPS - 1):
        low = interior_blocks(step, own // BLOCK)[0] * BLOCK
        if step % 2 == 0:
            high = low + BLOCK + REACH
        else:
            high = low + REACH
        if side:
            low, high = own - high, own - low
        at = HALO - bases[1]
        bufs[step % 4][:, at + low : at + high] = owns[step % 4][:, low:high]


def left_kernel(left, inner, done, own0, own1, own2, own3, state, seam, outer, buf0, buf1, buf2, buf3):
    own = done.shape[1]
    bases = (0, -REACH)
    bufs = (buf0, buf1, buf2, buf3)
    fringe = HALO // BLOCK
    middle = fringe + own // BLOCK // 2
    state[:, HALO:] = done[:, 0 : own // 2]
    edge = jnp.zeros((224, REACH), jnp.bfloat16)
    buf0[:, 0:REACH] = edge
    buf2[:, 2 * REACH : 3 * REACH] = edge
    carry_over((own0, own1, own2, own3), bufs, 0, bases)
    load_halo(left, 0, state, outer, buf0, bases)
    for step in range(1, STEPS + 1):
        inside = interior_blocks(step, own // BLOCK)
        stop = fringe + inside[0] if len(inside) else middle - (step == STEPS)
        places = [
            (
                block * BLOCK, BLOCK,
                functools.partial(lambda b: outer[b] if b < fringe else inner[b - fringe], block), True,
            )
            for block in range(step // 2, stop)
        ]
        sweep(state, bufs[(step - 1) % 4], bufs[step % 4] if step < STEPS else None, bases, places)
    low = (middle - 1) * BLOCK - REACH - bases[1]
    seam[...] = bufs[(STEPS - 1) % 4][:, low : low + BLOCK + REACH]


def right_kernel(
    ids, right, head, tail, root, ens, west, seam, inner, done, own0, own1, own2, own3,
    keep, send, state, outer, buf0, buf1, buf2, buf3, square, rowed,
):
    own = done.shape[1]
    wide = own + 2 * HALO
    tiles = own // LANES
    blocks = wide // BLOCK
    fringe = HALO // BLOCK
    middle = blocks // 2
    bases = ((middle - 1) * BLOCK, (middle - 2) * BLOCK)
    bufs = (buf0, buf1, buf2, buf3)
    state[:, 0:BLOCK] = west[:, (middle - 1) * BLOCK :]
    state[:, BLOCK : BLOCK + own // 2] = done[:, own // 2 :]
    edge = jnp.zeros((224, REACH), jnp.bfloat16)
    buf0[:, wide - bases[1] :] = edge
    buf2[:, wide - 2 * REACH - bases[1] : wide - REACH - bases[1]] = edge
    carry_over((own0, own1, own2, own3), bufs, 1, bases)
    load_halo(right, HALO + own, state, outer, buf0, bases)
    for step in range(1, STEPS + 1):
        inside = interior_blocks(step, own // BLOCK)
        start = fringe + inside[-1] + 1 if len(inside) else middle - (step == STEPS)
        places = [
            (
                block * BLOCK, BLOCK,
                functools.partial(
                    lambda b: inner[b - fringe] if b < blocks - fringe else outer[b - (blocks - fringe)], block
                ), True,
            )
            for block in range(start, blocks - step // 2)
        ]
        if step == STEPS:
            low = (middle - 1) * BLOCK - REACH - bases[1]
            bufs[(step - 1) % 4][:, low : low + BLOCK + REACH] = seam[...]
        sweep(state, bufs[(step - 1) % 4], bufs[step % 4] if step < STEPS else None, bases, places)

    square[...] = jnp.zeros(square.shape, jnp.float32)
    square[0:LEVELS, 0:LEVELS] = root[...]
    matrix = lax.dot_general(
        square[...], square[...], (((1,), (1,)), ((), ())),
        precision=lax.Precision.HIGHEST, preferred_element_type=jnp.float32,
    )
    matrix_high = matrix.astype(jnp.bfloat16)
    matrix_low = (matrix - matrix_high.astype(jnp.float32)).astype(jnp.bfloat16)
    stacked = jnp.concatenate([matrix_high, matrix_low], axis=0)
    total = jnp.zeros((1, BLOCK), jnp.float32)
    for block in range(own // BLOCK):
        at = (fringe + block) * BLOCK
        value = west[:, at : at + BLOCK] if at < bases[0] else state[:, at - bases[0] : at - bases[0] + BLOCK]
        high = value.astype(jnp.bfloat16)
        low = (value - high.astype(jnp.float32)).astype(jnp.bfloat16)
        first = jnp.dot(stacked, high, preferred_element_type=jnp.float32)
        second = jnp.dot(matrix_high, low, preferred_element_type=jnp.float32)
        smoothed = first[0:LEVELS] + (first[64 : 64 + LEVELS] + second[0:LEVELS])
        source = head if block < own // BLOCK // 2 else tail
        at = (block * BLOCK) % head.shape[1]
        total = total + jnp.sum(source[0:LEVELS, at : at + BLOCK] * smoothed, axis=0, keepdims=True)
        for tile in range(BLOCK // LANES):
            spot = block * (BLOCK // LANES) + tile
            rowed[pl.ds(spot, LEVELS, stride=tiles), :] = smoothed[:, tile * LANES : (tile + 1) * LANES]
    slots = 4
    chunk = rowed.shape[0] // slots
    spot = pl.ds(slots * chunk, 8)
    keep[spot, :] = send[spot, :] = jnp.broadcast_to(jnp.sum(total, axis=1, keepdims=True), (8, LANES))

    mine, chip = ids[0], ids[1]
    spare = slots * chunk - LEVELS * tiles

    def products(slot, start, first, count):
        rows = rowed[pl.ds(pl.multiple_of(start + first, 8), count), :]
        at = 2 * (start + first)
        here = pl.ds(slot * chunk + first, count)
        keep[here, :] = ens[pl.ds(at + mine, count, stride=2), :] * rows
        send[here, :] = ens[pl.ds(at + 1 - mine, count, stride=2), :] * rows

    for slot in range(slots):
        target = lax.rem(chip + slot, slots)
        start = target * chunk
        products(slot, start, 0, chunk - spare)

        @pl.when(target < slots - 1)
        def _():
            products(slot, start, chunk - spare, spare)

        @pl.when(target == slots - 1)
        def _():
            nothing = jnp.zeros((spare, LANES), jnp.float32)
            keep[pl.ds((slot + 1) * chunk - spare, spare), :] = nothing
            send[pl.ds((slot + 1) * chunk - spare, spare), :] = nothing


def place_pieces(ids, slots, same, other, out, lines, sems):
    mine, chip = ids[0], ids[1]
    chunk = lines.shape[0] // len(slots) // 2
    short = 2 * chunk - (4 * 2 * chunk - out.shape[0])
    waits = []
    for index, slot in enumerate(slots):
        source = lax.rem(chip + 4 - slot, 4)
        start = index * 2 * chunk
        lines[pl.ds(start + mine, chunk, stride=2), :] = same[index, 0:chunk, :]
        lines[pl.ds(start + 1 - mine, chunk, stride=2), :] = other[index, 0:chunk, :]
        target = pl.multiple_of(source * 2 * chunk, 8)
        main = pltpu.make_async_copy(
            lines.at[pl.ds(start, short)], out.at[pl.ds(target, short)], sems.at[0, index]
        )
        extra = pltpu.make_async_copy(
            lines.at[pl.ds(start + short, 2 * chunk - short)],
            out.at[pl.ds(pl.multiple_of(target + short, 8), 2 * chunk - short)],
            sems.at[1, index],
        )
        main.start()
        pl.when(source < 3)(extra.start)
        waits.append((source, main, extra))
    return waits


def wait_pieces(waits):
    for source, main, extra in waits:
        main.wait()
        pl.when(source < 3)(extra.wait)


def early_kernel(ids, same, other, out, lines, sems):
    wait_pieces(place_pieces(ids, EARLY, same, other, out, lines, sems))


def late_kernel(scale, ids, begun, early, same, other, out, quadratic, lines, sems):
    waits = place_pieces(ids, LATE, same, other, out, lines, sems)
    chunk = lines.shape[0] // len(LATE) // 2
    near, far = [
        pieces[0, chunk : chunk + 8, :] + pieces[1, chunk : chunk + 8, :] for pieces in (early, same)
    ]
    quadratic[0, 0] = jnp.max(near + far) * scale
    wait_pieces(waits)


def interleave(array):
    cells = array.shape[2]
    array = array.reshape(2, LEVELS, cells // LANES, LANES)
    return array.transpose(1, 2, 0, 3).reshape(-1, LANES)


def on_device(ensemble, field, diffusivity, neighbours, vertical_root):
    own = diffusivity.shape[0]
    patches = lax.axis_size("patch")
    members = lax.axis_size("mem")
    chips = members // 2
    all_cells = own * patches
    half = own // 2
    tiles = own // LANES
    vmem = pl.BlockSpec(memory_space=pltpu.VMEM)
    smem = pl.BlockSpec(memory_space=pltpu.SMEM)
    hbm = pl.BlockSpec(memory_space=pltpu.HBM)
    params = pltpu.CompilerParams(vmem_limit_bytes=32 * 1024 * 1024)
    place = (lax.axis_index("patch") * own).astype(jnp.int32).reshape(1)
    member = lax.axis_index("mem")
    ids = jnp.stack([lax.rem(member, 2), member // 2]).astype(jnp.int32)
    ens_rows = interleave(ensemble[0])
    field_rows = interleave(field)

    in_hbm = [
        pltpu.with_memory_space_constraint(array, pltpu.HBM)
        for array in (ens_rows, field_rows, diffusivity.reshape(1, own), neighbours)
    ]
    side = jax.ShapeDtypeStruct((64, half), jnp.float32)
    head, tail = pl.pallas_call(
        functools.partial(prepare_kernel, all_cells),
        out_shape=(side, side),
        in_specs=[smem, hbm, hbm, hbm, hbm],
        out_specs=(vmem, vmem),
        scratch_shapes=[
            pltpu.VMEM(ens_rows.shape, jnp.float32),
            pltpu.VMEM(ens_rows.shape, jnp.float32),
            pltpu.VMEM((1, own), jnp.float32),
            pltpu.VMEM((7, own), jnp.int32),
            pltpu.SemaphoreType.DMA((3, 4)),
        ],
        compiler_params=params,
        name="prepare",
    )(place, *in_hbm)

    left = lax.ppermute(tail, "patch", [(i, (i + 1) % patches) for i in range(patches)])
    right = lax.ppermute(head, "patch", [((i + 1) % patches, i) for i in range(patches)])

    parts = jax.ShapeDtypeStruct((224, own), jnp.bfloat16)
    inside = pl.pallas_call(
        interior_kernel,
        out_shape=(
            jax.ShapeDtypeStruct((own // BLOCK, 2 * BLOCK, BLOCK), jnp.bfloat16),
            jax.ShapeDtypeStruct((64, own), jnp.float32),
            parts, parts, parts, parts,
        ),
        in_specs=[vmem] * 2,
        out_specs=(vmem,) * 6,
        compiler_params=params,
        cost_estimate=pl.CostEstimate(flops=0, bytes_accessed=7_000_000, transcendentals=0),
        name="interior",
    )(head, tail)

    chunk = 56 * tiles // chips
    west, seam = pl.pallas_call(
        left_kernel,
        out_shape=(
            jax.ShapeDtypeStruct((64, HALO + half), jnp.float32),
            jax.ShapeDtypeStruct((224, BLOCK + REACH), jnp.bfloat16),
        ),
        in_specs=[vmem] * 7,
        out_specs=(vmem,) * 2,
        scratch_shapes=[pltpu.VMEM((HALO // BLOCK, 2 * BLOCK, BLOCK), jnp.bfloat16)]
        + [pltpu.VMEM((224, HALO + half + 2 * REACH), jnp.bfloat16)] * 4,
        compiler_params=params,
        cost_estimate=pl.CostEstimate(flops=0, bytes_accessed=7_000_000, transcendentals=0),
        name="left",
    )(left, *inside)
    terms = jax.ShapeDtypeStruct((chips * chunk + 8, LANES), jnp.float32)
    keep, send = pl.pallas_call(
        right_kernel,
        out_shape=(terms, terms),
        in_specs=[smem] + [vmem] * 13,
        out_specs=(vmem, vmem),
        scratch_shapes=[
            pltpu.VMEM((64, BLOCK + half + HALO), jnp.float32),
            pltpu.VMEM((HALO // BLOCK, 2 * BLOCK, BLOCK), jnp.bfloat16),
        ]
        + [pltpu.VMEM((224, 2 * BLOCK + half + HALO + REACH), jnp.bfloat16)] * 4
        + [
            pltpu.VMEM((64, 64), jnp.float32),
            pltpu.VMEM((56 * tiles, LANES), jnp.float32),
        ],
        compiler_params=params,
        cost_estimate=pl.CostEstimate(flops=0, bytes_accessed=7_000_000, transcendentals=0),
        name="right",
    )(ids, right, head, tail, vertical_root, ens_rows, west, seam, *inside)

    def shift_chips(array, by):
        pairs = [(2 * z + c, 2 * ((z + by) % chips) + c) for z in range(chips) for c in range(2)]
        return lax.ppermute(array, "mem", pairs)

    twin = [(i, i ^ 1) for i in range(members)]
    order = [2, 1, 3]
    pair_sum = keep + lax.ppermute(send, "mem", twin)
    pieces = [pair_sum[chunk * slot : chunk * (slot + 1)] for slot in range(chips)]
    terms = {by: shift_chips(pieces[by], by) for by in order}
    spread = jnp.broadcast_to(pair_sum[chips * chunk : chips * chunk + 1][None], (patches, 1, LANES))
    spread = lax.all_to_all(spread, "patch", 0, 0)
    terms, spread = lax.optimization_barrier((terms, spread))
    total = (pieces[0] + terms[1] + terms[2] + terms[3]) / (members - 1.0)
    total = jnp.concatenate([total, jnp.broadcast_to(jnp.sum(spread, axis=0), (8, LANES))], axis=0)
    copies = {by: shift_chips(total, by) for by in order}
    sources = {0: total, **copies}
    scale = 1.0 / ((members - 1.0) * field.shape[0] * field.shape[1] * all_cells)
    scratch = [
        pltpu.VMEM((2 * chunk * 2, LANES), jnp.float32),
        pltpu.SemaphoreType.DMA((2, 2)),
    ]
    early = jnp.stack([sources[by] for by in EARLY])
    rows = pl.pallas_call(
        early_kernel,
        out_shape=jax.ShapeDtypeStruct(field_rows.shape, jnp.float32),
        in_specs=[smem, vmem, vmem],
        out_specs=hbm,
        scratch_shapes=scratch,
        compiler_params=params,
        cost_estimate=pl.CostEstimate(flops=1_000_000, bytes_accessed=4_000_000, transcendentals=0),
        name="early",
    )(ids, early, lax.ppermute(early, "mem", twin))
    late = jnp.stack([sources[by] for by in LATE])
    rows, quadratic = pl.pallas_call(
        functools.partial(late_kernel, scale),
        out_shape=(
            jax.ShapeDtypeStruct(field_rows.shape, jnp.float32),
            jax.ShapeDtypeStruct((1, 1), jnp.float32),
        ),
        in_specs=[smem, hbm, vmem, vmem, vmem],
        out_specs=(hbm, smem),
        scratch_shapes=scratch,
        input_output_aliases={1: 0},
        compiler_params=params,
        name="late",
    )(ids, rows, early, late, lax.ppermute(late, "mem", twin))
    product = rows.reshape(LEVELS, tiles, 2, LANES).transpose(2, 0, 1, 3).reshape(field.shape)
    return (product, quadratic.reshape(()))


def solution(mesh):
    return jax.shard_map(
        on_device,
        mesh=mesh,
        in_specs=(
            P("mem", None, None, "patch"),
            P(None, None, "patch"),
            P("patch"),
            P(None, "patch"),
            P(),
        ),
        out_specs=(P(None, None, "patch"), P()),
        check_vma=False,
    )
```

```python
import functools

import jax
import jax.numpy as jnp
from jax import lax
from jax.experimental import pallas as pl
from jax.experimental.pallas import tpu as pltpu
from jax.sharding import PartitionSpec as P

STEPS = 8
REACH = 128
BLOCK = 256
HALO = STEPS * REACH
LEVELS = 55
LANES = 128
EARLY, LATE = (0, 2), (1, 3)


def prepare_kernel(
    all_cells, place, ens, field, diff, neigh, head, tail, ens_in, field_in, diff_in, neigh_in, sems
):
    own = diff.shape[1]
    tiles = own // LANES
    half = own // 2
    start = place[0]
    levels = (0, 16, 32, 48, LEVELS)
    copies = []
    for turn in range(4):
        rows = pl.ds(levels[turn] * 2 * tiles, (levels[turn + 1] - levels[turn]) * 2 * tiles)
        copies.append((
            pltpu.make_async_copy(ens.at[rows], ens_in.at[rows], sems.at[0, turn]),
            pltpu.make_async_copy(field.at[rows], field_in.at[rows], sems.at[1, turn]),
        ))
    others = (
        pltpu.make_async_copy(neigh, neigh_in, sems.at[2, 0]),
        pltpu.make_async_copy(diff, diff_in, sems.at[2, 1]),
    )
    for copy in others + copies[0] + copies[1] + copies[2] + copies[3]:
        copy.start()
    for copy in others:
        copy.wait()
    for part, out in ((0, head), (1, tail)):
        cols = pl.ds(part * half, half)
        out[55:56, :] = jnp.ones((1, half), jnp.float32)
        cell = lax.broadcasted_iota(jnp.int32, (7, half), 1) + (start + part * half)
        shift = neigh_in[:, cols] - cell
        shift = jnp.where(shift > all_cells // 2, shift - all_cells, shift)
        shift = jnp.where(shift < -(all_cells // 2), shift + all_cells, shift)
        out[56:63, :] = shift.astype(jnp.float32)
        out[63:64, :] = diff_in[:, cols]
    for turn in range(4):
        for copy in copies[turn]:
            copy.wait()
        low, high = levels[turn], levels[turn + 1]
        rows = pl.ds(low * 2 * tiles, (high - low) * 2 * tiles)
        ens_in[rows, :] = ens_in[rows, :] * field_in[rows, :]
        for part, out in ((0, head), (1, tail)):
            for tile in range(tiles // 2):
                at = low * 2 * tiles + 2 * (part * (tiles // 2) + tile)
                out[low:high, tile * LANES : (tile + 1) * LANES] = (
                    ens_in[pl.ds(at, high - low, stride=2 * tiles), :]
                    + ens_in[pl.ds(at + 1, high - low, stride=2 * tiles), :]
                )


def build_block(shift, store):
    row = lax.broadcasted_iota(jnp.int32, (LANES, LANES), 0).astype(jnp.float32).astype(jnp.bfloat16)
    lane = lax.broadcasted_iota(jnp.int32, (1, LANES), 1).astype(jnp.float32)
    one = jnp.ones((LANES, LANES), jnp.bfloat16)
    zero = jnp.zeros((LANES, LANES), jnp.bfloat16)
    for chunk in range(BLOCK // LANES):
        part = shift[:, chunk * LANES : (chunk + 1) * LANES]
        for side in range(3):
            local = part + (lane + (1.0 - side) * LANES)
            inside = jnp.logical_and(jnp.logical_and(local >= 0.0, local < LANES), part != 0.0)
            local = jnp.where(inside, local, -1.0).astype(jnp.bfloat16)
            hit = zero
            for slot in range(7):
                hit = jnp.where(row == local[slot : slot + 1, :], one, hit)
            store(chunk + side, chunk, hit)
        store((chunk + 3) % 4, chunk, zero)


def split(value, coeff):
    both = jnp.concatenate([value, coeff * value], axis=0)
    high = both.astype(jnp.bfloat16)
    low = (both - high.astype(jnp.float32)).astype(jnp.bfloat16)
    return high, low


def store_parts(buf, at, parts):
    width = parts[0].shape[1]
    buf[0:112, at : at + width] = parts[0]
    buf[112:224, at : at + width] = parts[1]


def sweep(state, now, later, bases, places):
    first, origin = bases

    def matmul(at, width, matrix):
        low = at - origin - REACH
        return jnp.dot(now[:, low : low + width + 2 * REACH], matrix, preferred_element_type=jnp.float32)

    def finish(at, width, kept, total):
        here = slice(at - first, at - first + width)
        coeff = state[56:57, here]
        value = state[0:56, here]
        change = coeff * (total[0:56] + total[112:168]) + (total[56:112] + total[168:224])
        value = value * (1.0 - change[55:56]) + change
        if kept:
            state[0:56, here] = value
        if later is not None:
            store_parts(later, at - origin, split(value, coeff))

    waiting = None
    for at, width, matrix, kept in places:
        total = matmul(at, width, matrix())
        if waiting is not None:
            finish(*waiting)
        waiting = (at, width, kept, total)
    finish(*waiting)


def interior_blocks(step, count):
    skip = (step + 1) // 2
    return range(skip, count - skip)


def seams(own, side):
    packed = 0
    for step in range(STEPS - 1):
        low = interior_blocks(step, own // BLOCK)[0] * BLOCK
        high = low + REACH + (BLOCK if step % 2 == 0 else 0)
        if side:
            yield step, own - high, own - low, packed
        else:
            yield step, low, high, packed
        packed += high - low


def packed_columns(own):
    return sum(high - low for _, low, high, _ in seams(own, 0))


def interior_kernel(
    head, tail, near_adj, far_adj, near_state, far_state, near_parts, far_parts, values,
    adj, state, buf0, buf1, buf2, buf3,
):
    bufs = (buf0, buf1, buf2, buf3)
    blocks = adj.shape[0]
    own = blocks * BLOCK
    half = blocks // 2
    for block in range(blocks):
        source, at = (head, block * BLOCK) if block < half else (tail, (block - half) * BLOCK)

        def store(down, across, value):
            spot = (slice(down * LANES, (down + 1) * LANES), slice(across * LANES, (across + 1) * LANES))
            adj[block, *spot] = value
            if block < half:
                near_adj[block, *spot] = value
            if block >= half - 1:
                far_adj[block - (half - 1), *spot] = value

        value = source[:, at : at + BLOCK]
        build_block(value[56:63], store)
        coeff = 0.5 * value[63:64]
        here = block * BLOCK
        state[0:56, here : here + BLOCK] = value[0:56]
        state[56:64, here : here + BLOCK] = jnp.broadcast_to(coeff, (8, BLOCK))
        values[:, here : here + BLOCK] = value[0:56]
        store_parts(buf0, here, split(value[0:56], coeff))
    for step in range(1, STEPS - 1):
        whole = interior_blocks(step, blocks)
        places = [(block * BLOCK, BLOCK, functools.partial(lambda b: adj[b], block), True) for block in whole]
        if step % 2:
            low, high = whole[0] - 1, whole[-1] + 1
            places.append((low * BLOCK + REACH, REACH, lambda: adj[low, REACH:, REACH:], False))
            places.append((high * BLOCK, REACH, lambda: adj[high, : BLOCK + REACH, :REACH], False))
        sweep(state, bufs[(step - 1) % 4], bufs[step % 4], (0, 0), places)
    near_state[...] = state[:, 0 : own // 2]
    far_state[...] = state[:, own // 2 :]
    for side, parts in ((0, near_parts), (1, far_parts)):
        for step, low, high, packed in seams(own, side):
            parts[:, packed : packed + high - low] = bufs[step % 4][:, low:high]


def load_halo(part, at, state, outer, buf, bases):
    for index in range(HALO // BLOCK):
        value = part[:, index * BLOCK : (index + 1) * BLOCK]
        coeff = 0.5 * value[63:64]
        here = at + index * BLOCK
        spot = slice(here - bases[0], here - bases[0] + BLOCK)
        state[0:56, spot] = value[0:56]
        state[56:64, spot] = jnp.broadcast_to(coeff, (8, BLOCK))
        store_parts(buf, here - bases[1], split(value[0:56], coeff))

        def store(down, across, piece):
            outer[index, down * LANES : (down + 1) * LANES, across * LANES : (across + 1) * LANES] = piece

        build_block(value[56:63], store)


def carry_over(parts, bufs, own, side, bases):
    at = HALO - bases[1]
    for step, low, high, packed in seams(own, side):
        bufs[step % 4][:, at + low : at + high] = parts[:, packed : packed + high - low]


def left_kernel(left, inner, done, parts, state, seam, outer, buf0, buf1, buf2, buf3):
    own = 2 * done.shape[1]
    bases = (0, -REACH)
    bufs = (buf0, buf1, buf2, buf3)
    fringe = HALO // BLOCK
    middle = fringe + own // BLOCK // 2
    state[:, HALO:] = done[...]
    edge = jnp.zeros((224, REACH), jnp.bfloat16)
    buf0[:, 0:REACH] = edge
    buf2[:, 2 * REACH : 3 * REACH] = edge
    carry_over(parts, bufs, own, 0, bases)
    load_halo(left, 0, state, outer, buf0, bases)
    for step in range(1, STEPS + 1):
        inside = interior_blocks(step, own // BLOCK)
        stop = fringe + inside[0] if len(inside) else middle - (step == STEPS)
        places = [
            (
                block * BLOCK, BLOCK,
                functools.partial(lambda b: outer[b] if b < fringe else inner[b - fringe], block), True,
            )
            for block in range(step // 2, stop)
        ]
        sweep(state, bufs[(step - 1) % 4], bufs[step % 4] if step < STEPS else None, bases, places)
    low = (middle - 1) * BLOCK - REACH - bases[1]
    seam[...] = bufs[(STEPS - 1) % 4][:, low : low + BLOCK + REACH]


def right_kernel(
    ids, right, root, ens, west, seam, inner, done, parts, values,
    keep, send, state, outer, buf0, buf1, buf2, buf3, square, rowed,
):
    own = 2 * done.shape[1]
    wide = own + 2 * HALO
    tiles = own // LANES
    blocks = wide // BLOCK
    fringe = HALO // BLOCK
    middle = blocks // 2
    bases = ((middle - 1) * BLOCK, (middle - 2) * BLOCK)
    bufs = (buf0, buf1, buf2, buf3)
    state[:, 0:BLOCK] = west[:, (middle - 1) * BLOCK :]
    state[:, BLOCK : BLOCK + own // 2] = done[...]
    edge = jnp.zeros((224, REACH), jnp.bfloat16)
    buf0[:, wide - bases[1] :] = edge
    buf2[:, wide - 2 * REACH - bases[1] : wide - REACH - bases[1]] = edge
    carry_over(parts, bufs, own, 1, bases)
    load_halo(right, HALO + own, state, outer, buf0, bases)
    for step in range(1, STEPS + 1):
        inside = interior_blocks(step, own // BLOCK)
        start = fringe + inside[-1] + 1 if len(inside) else middle - (step == STEPS)
        places = [
            (
                block * BLOCK, BLOCK,
                functools.partial(
                    lambda b: inner[b - (middle - 1)] if b < blocks - fringe else outer[b - (blocks - fringe)], block
                ), True,
            )
            for block in range(start, blocks - step // 2)
        ]
        if step == STEPS:
            low = (middle - 1) * BLOCK - REACH - bases[1]
            bufs[(step - 1) % 4][:, low : low + BLOCK + REACH] = seam[...]
        sweep(state, bufs[(step - 1) % 4], bufs[step % 4] if step < STEPS else None, bases, places)

    square[...] = jnp.zeros(square.shape, jnp.float32)
    square[0:LEVELS, 0:LEVELS] = root[...]
    matrix = lax.dot_general(
        square[...], square[...], (((1,), (1,)), ((), ())),
        precision=lax.Precision.HIGHEST, preferred_element_type=jnp.float32,
    )
    matrix_high = matrix.astype(jnp.bfloat16)
    matrix_low = (matrix - matrix_high.astype(jnp.float32)).astype(jnp.bfloat16)
    stacked = jnp.concatenate([matrix_high, matrix_low], axis=0)
    total = jnp.zeros((1, BLOCK), jnp.float32)
    for block in range(own // BLOCK):
        at = (fringe + block) * BLOCK
        value = west[:, at : at + BLOCK] if at < bases[0] else state[:, at - bases[0] : at - bases[0] + BLOCK]
        high = value.astype(jnp.bfloat16)
        low = (value - high.astype(jnp.float32)).astype(jnp.bfloat16)
        first = jnp.dot(stacked, high, preferred_element_type=jnp.float32)
        second = jnp.dot(matrix_high, low, preferred_element_type=jnp.float32)
        smoothed = first[0:LEVELS] + (first[64 : 64 + LEVELS] + second[0:LEVELS])
        at = block * BLOCK
        total = total + jnp.sum(values[0:LEVELS, at : at + BLOCK] * smoothed, axis=0, keepdims=True)
        for tile in range(BLOCK // LANES):
            spot = block * (BLOCK // LANES) + tile
            rowed[pl.ds(spot, LEVELS, stride=tiles), :] = smoothed[:, tile * LANES : (tile + 1) * LANES]
    slots = 4
    chunk = rowed.shape[0] // slots
    spot = pl.ds(slots * chunk, 8)
    keep[spot, :] = send[spot, :] = jnp.broadcast_to(jnp.sum(total, axis=1, keepdims=True), (8, LANES))

    mine, chip = ids[0], ids[1]
    spare = slots * chunk - LEVELS * tiles

    def products(slot, start, first, count):
        rows = rowed[pl.ds(pl.multiple_of(start + first, 8), count), :]
        at = 2 * (start + first)
        here = pl.ds(slot * chunk + first, count)
        keep[here, :] = ens[pl.ds(at + mine, count, stride=2), :] * rows
        send[here, :] = ens[pl.ds(at + 1 - mine, count, stride=2), :] * rows

    for slot in range(slots):
        target = lax.rem(chip + slot, slots)
        start = target * chunk
        products(slot, start, 0, chunk - spare)

        @pl.when(target < slots - 1)
        def _():
            products(slot, start, chunk - spare, spare)

        @pl.when(target == slots - 1)
        def _():
            nothing = jnp.zeros((spare, LANES), jnp.float32)
            keep[pl.ds((slot + 1) * chunk - spare, spare), :] = nothing
            send[pl.ds((slot + 1) * chunk - spare, spare), :] = nothing


def place_pieces(ids, slots, same, other, out, lines, sems):
    mine, chip = ids[0], ids[1]
    chunk = lines.shape[0] // len(slots) // 2
    short = 2 * chunk - (4 * 2 * chunk - out.shape[0])
    waits = []
    for index, slot in enumerate(slots):
        source = lax.rem(chip + 4 - slot, 4)
        start = index * 2 * chunk
        lines[pl.ds(start + mine, chunk, stride=2), :] = same[index, 0:chunk, :]
        lines[pl.ds(start + 1 - mine, chunk, stride=2), :] = other[index, 0:chunk, :]
        target = pl.multiple_of(source * 2 * chunk, 8)
        main = pltpu.make_async_copy(
            lines.at[pl.ds(start, short)], out.at[pl.ds(target, short)], sems.at[0, index]
        )
        extra = pltpu.make_async_copy(
            lines.at[pl.ds(start + short, 2 * chunk - short)],
            out.at[pl.ds(pl.multiple_of(target + short, 8), 2 * chunk - short)],
            sems.at[1, index],
        )
        main.start()
        pl.when(source < 3)(extra.start)
        waits.append((source, main, extra))
    return waits


def wait_pieces(waits):
    for source, main, extra in waits:
        main.wait()
        pl.when(source < 3)(extra.wait)


def early_kernel(ids, same, other, out, lines, sems):
    wait_pieces(place_pieces(ids, EARLY, same, other, out, lines, sems))


def late_kernel(scale, ids, begun, early, same, other, out, quadratic, lines, sems):
    waits = place_pieces(ids, LATE, same, other, out, lines, sems)
    chunk = lines.shape[0] // len(LATE) // 2
    near, far = [
        pieces[0, chunk : chunk + 8, :] + pieces[1, chunk : chunk + 8, :] for pieces in (early, same)
    ]
    quadratic[0, 0] = jnp.max(near + far) * scale
    wait_pieces(waits)


def interleave(array):
    cells = array.shape[2]
    array = array.reshape(2, LEVELS, cells // LANES, LANES)
    return array.transpose(1, 2, 0, 3).reshape(-1, LANES)


def on_device(ensemble, field, diffusivity, neighbours, vertical_root):
    own = diffusivity.shape[0]
    patches = lax.axis_size("patch")
    members = lax.axis_size("mem")
    chips = members // 2
    all_cells = own * patches
    half = own // 2
    tiles = own // LANES
    vmem = pl.BlockSpec(memory_space=pltpu.VMEM)
    smem = pl.BlockSpec(memory_space=pltpu.SMEM)
    hbm = pl.BlockSpec(memory_space=pltpu.HBM)
    params = pltpu.CompilerParams(vmem_limit_bytes=32 * 1024 * 1024)
    place = (lax.axis_index("patch") * own).astype(jnp.int32).reshape(1)
    member = lax.axis_index("mem")
    ids = jnp.stack([lax.rem(member, 2), member // 2]).astype(jnp.int32)
    ens_rows = interleave(ensemble[0])
    field_rows = interleave(field)

    in_hbm = [
        pltpu.with_memory_space_constraint(array, pltpu.HBM)
        for array in (ens_rows, field_rows, diffusivity.reshape(1, own), neighbours)
    ]
    side = jax.ShapeDtypeStruct((64, half), jnp.float32)
    head, tail = pl.pallas_call(
        functools.partial(prepare_kernel, all_cells),
        out_shape=(side, side),
        in_specs=[smem, hbm, hbm, hbm, hbm],
        out_specs=(vmem, vmem),
        scratch_shapes=[
            pltpu.VMEM(ens_rows.shape, jnp.float32),
            pltpu.VMEM(ens_rows.shape, jnp.float32),
            pltpu.VMEM((1, own), jnp.float32),
            pltpu.VMEM((7, own), jnp.int32),
            pltpu.SemaphoreType.DMA((3, 4)),
        ],
        compiler_params=params,
        name="prepare",
    )(place, *in_hbm)

    left = lax.ppermute(tail, "patch", [(i, (i + 1) % patches) for i in range(patches)])
    right = lax.ppermute(head, "patch", [((i + 1) % patches, i) for i in range(patches)])

    blocks = own // BLOCK
    adjacency = (2 * BLOCK, BLOCK)
    packed = jax.ShapeDtypeStruct((224, packed_columns(own)), jnp.bfloat16)
    half_state = jax.ShapeDtypeStruct((64, half), jnp.float32)
    near_adj, far_adj, near_state, far_state, near_parts, far_parts, values = pl.pallas_call(
        interior_kernel,
        out_shape=(
            jax.ShapeDtypeStruct((blocks // 2, *adjacency), jnp.bfloat16),
            jax.ShapeDtypeStruct((blocks // 2 + 1, *adjacency), jnp.bfloat16),
            half_state, half_state, packed, packed,
            jax.ShapeDtypeStruct((56, own), jnp.float32),
        ),
        in_specs=[vmem] * 2,
        out_specs=(vmem,) * 7,
        scratch_shapes=[pltpu.VMEM((blocks, *adjacency), jnp.bfloat16), pltpu.VMEM((64, own), jnp.float32)]
        + [pltpu.VMEM((224, own), jnp.bfloat16)] * 4,
        compiler_params=params,
        cost_estimate=pl.CostEstimate(flops=0, bytes_accessed=7_000_000, transcendentals=0),
        name="interior",
    )(head, tail)

    chunk = 56 * tiles // chips
    west, seam = pl.pallas_call(
        left_kernel,
        out_shape=(
            jax.ShapeDtypeStruct((64, HALO + half), jnp.float32),
            jax.ShapeDtypeStruct((224, BLOCK + REACH), jnp.bfloat16),
        ),
        in_specs=[vmem] * 4,
        out_specs=(vmem,) * 2,
        scratch_shapes=[pltpu.VMEM((HALO // BLOCK, 2 * BLOCK, BLOCK), jnp.bfloat16)]
        + [pltpu.VMEM((224, HALO + half + 2 * REACH), jnp.bfloat16)] * 4,
        compiler_params=params,
        cost_estimate=pl.CostEstimate(flops=0, bytes_accessed=7_000_000, transcendentals=0),
        name="left",
    )(left, near_adj, near_state, near_parts)
    terms = jax.ShapeDtypeStruct((chips * chunk + 8, LANES), jnp.float32)
    keep, send = pl.pallas_call(
        right_kernel,
        out_shape=(terms, terms),
        in_specs=[smem] + [vmem] * 9,
        out_specs=(vmem, vmem),
        scratch_shapes=[
            pltpu.VMEM((64, BLOCK + half + HALO), jnp.float32),
            pltpu.VMEM((HALO // BLOCK, 2 * BLOCK, BLOCK), jnp.bfloat16),
        ]
        + [pltpu.VMEM((224, 2 * BLOCK + half + HALO + REACH), jnp.bfloat16)] * 4
        + [
            pltpu.VMEM((64, 64), jnp.float32),
            pltpu.VMEM((56 * tiles, LANES), jnp.float32),
        ],
        compiler_params=params,
        cost_estimate=pl.CostEstimate(flops=0, bytes_accessed=7_000_000, transcendentals=0),
        name="right",
    )(ids, right, vertical_root, ens_rows, west, seam, far_adj, far_state, far_parts, values)

    def shift_chips(array, by):
        pairs = [(2 * z + c, 2 * ((z + by) % chips) + c) for z in range(chips) for c in range(2)]
        return lax.ppermute(array, "mem", pairs)

    twin = [(i, i ^ 1) for i in range(members)]
    order = [2, 1, 3]
    pair_sum = keep + lax.ppermute(send, "mem", twin)
    pieces = [pair_sum[chunk * slot : chunk * (slot + 1)] for slot in range(chips)]
    terms = {by: shift_chips(pieces[by], by) for by in order}
    spread = jnp.broadcast_to(pair_sum[chips * chunk : chips * chunk + 1][None], (patches, 1, LANES))
    spread = lax.all_to_all(spread, "patch", 0, 0)
    terms, spread = lax.optimization_barrier((terms, spread))
    total = (pieces[0] + terms[1] + terms[2] + terms[3]) / (members - 1.0)
    total = jnp.concatenate([total, jnp.broadcast_to(jnp.sum(spread, axis=0), (8, LANES))], axis=0)
    copies = {by: shift_chips(total, by) for by in order}
    sources = {0: total, **copies}
    scale = 1.0 / ((members - 1.0) * field.shape[0] * field.shape[1] * all_cells)
    scratch = [
        pltpu.VMEM((2 * chunk * 2, LANES), jnp.float32),
        pltpu.SemaphoreType.DMA((2, 2)),
    ]
    early = jnp.stack([sources[by] for by in EARLY])
    rows = pl.pallas_call(
        early_kernel,
        out_shape=jax.ShapeDtypeStruct(field_rows.shape, jnp.float32),
        in_specs=[smem, vmem, vmem],
        out_specs=hbm,
        scratch_shapes=scratch,
        compiler_params=params,
        cost_estimate=pl.CostEstimate(flops=1_000_000, bytes_accessed=4_000_000, transcendentals=0),
        name="early",
    )(ids, early, lax.ppermute(early, "mem", twin))
    late = jnp.stack([sources[by] for by in LATE])
    rows, quadratic = pl.pallas_call(
        functools.partial(late_kernel, scale),
        out_shape=(
            jax.ShapeDtypeStruct(field_rows.shape, jnp.float32),
            jax.ShapeDtypeStruct((1, 1), jnp.float32),
        ),
        in_specs=[smem, hbm, vmem, vmem, vmem],
        out_specs=(hbm, smem),
        scratch_shapes=scratch,
        input_output_aliases={1: 0},
        compiler_params=params,
        name="late",
    )(ids, rows, early, late, lax.ppermute(late, "mem", twin))
    product = rows.reshape(LEVELS, tiles, 2, LANES).transpose(2, 0, 1, 3).reshape(field.shape)
    return (product, quadratic.reshape(()))


def solution(mesh):
    return jax.shard_map(
        on_device,
        mesh=mesh,
        in_specs=(
            P("mem", None, None, "patch"),
            P(None, None, "patch"),
            P("patch"),
            P(None, "patch"),
            P(),
        ),
        out_specs=(P(None, None, "patch"), P()),
        check_vma=False,
    )
```

```python
import functools

import jax
import jax.numpy as jnp
from jax import lax
from jax.experimental import pallas as pl
from jax.experimental.pallas import tpu as pltpu
from jax.sharding import PartitionSpec as P

STEPS = 8
REACH = 128
BLOCK = 256
HALO = STEPS * REACH
LEVELS = 55
LANES = 128
EARLY, LATE = (0, 2), (1, 3)


def prepare_kernel(
    all_cells, place, ens, field, diff, neigh, head, tail, ens_in, field_in, diff_in, neigh_in, sems
):
    own = diff.shape[1]
    tiles = own // LANES
    half = own // 2
    start = place[0]
    levels = (0, 16, 32, 48, LEVELS)
    copies = []
    for turn in range(4):
        rows = pl.ds(levels[turn] * 2 * tiles, (levels[turn + 1] - levels[turn]) * 2 * tiles)
        copies.append((
            pltpu.make_async_copy(ens.at[rows], ens_in.at[rows], sems.at[0, turn]),
            pltpu.make_async_copy(field.at[rows], field_in.at[rows], sems.at[1, turn]),
        ))
    others = (
        pltpu.make_async_copy(neigh, neigh_in, sems.at[2, 0]),
        pltpu.make_async_copy(diff, diff_in, sems.at[2, 1]),
    )
    for copy in others + copies[0] + copies[1] + copies[2] + copies[3]:
        copy.start()
    for copy in others:
        copy.wait()
    for part, out in ((0, head), (1, tail)):
        cols = pl.ds(part * half, half)
        out[55:56, :] = jnp.ones((1, half), jnp.float32)
        cell = lax.broadcasted_iota(jnp.int32, (7, half), 1) + (start + part * half)
        shift = neigh_in[:, cols] - cell
        shift = jnp.where(shift > all_cells // 2, shift - all_cells, shift)
        shift = jnp.where(shift < -(all_cells // 2), shift + all_cells, shift)
        out[56:63, :] = shift.astype(jnp.float32)
        out[63:64, :] = diff_in[:, cols]
    for turn in range(4):
        for copy in copies[turn]:
            copy.wait()
        low, high = levels[turn], levels[turn + 1]
        rows = pl.ds(low * 2 * tiles, (high - low) * 2 * tiles)
        ens_in[rows, :] = ens_in[rows, :] * field_in[rows, :]
        for part, out in ((0, head), (1, tail)):
            for tile in range(tiles // 2):
                at = low * 2 * tiles + 2 * (part * (tiles // 2) + tile)
                out[low:high, tile * LANES : (tile + 1) * LANES] = (
                    ens_in[pl.ds(at, high - low, stride=2 * tiles), :]
                    + ens_in[pl.ds(at + 1, high - low, stride=2 * tiles), :]
                )


def build_block(shift, store):
    row = lax.broadcasted_iota(jnp.int32, (LANES, LANES), 0).astype(jnp.float32).astype(jnp.bfloat16)
    lane = lax.broadcasted_iota(jnp.int32, (1, LANES), 1).astype(jnp.float32)
    one = jnp.ones((LANES, LANES), jnp.bfloat16)
    zero = jnp.zeros((LANES, LANES), jnp.bfloat16)
    for chunk in range(BLOCK // LANES):
        part = shift[:, chunk * LANES : (chunk + 1) * LANES]
        for side in range(3):
            local = part + (lane + (1.0 - side) * LANES)
            inside = jnp.logical_and(jnp.logical_and(local >= 0.0, local < LANES), part != 0.0)
            local = jnp.where(inside, local, -1.0).astype(jnp.bfloat16)
            hit = zero
            for slot in range(7):
                hit = jnp.where(row == local[slot : slot + 1, :], one, hit)
            store(chunk + side, chunk, hit)
        store((chunk + 3) % 4, chunk, zero)


def split(value, coeff):
    both = jnp.concatenate([value, coeff * value], axis=0)
    high = both.astype(jnp.bfloat16)
    low = (both - high.astype(jnp.float32)).astype(jnp.bfloat16)
    return high, low


def store_parts(buf, at, parts):
    width = parts[0].shape[1]
    buf[0:112, at : at + width] = parts[0]
    buf[112:224, at : at + width] = parts[1]


def sweep(state, now, later, bases, places):
    first, origin = bases

    def matmul(at, width, matrix):
        low = at - origin - REACH
        return jnp.dot(now[:, low : low + width + 2 * REACH], matrix, preferred_element_type=jnp.float32)

    def finish(at, width, kept, total):
        here = slice(at - first, at - first + width)
        coeff = state[56:57, here]
        value = state[0:56, here]
        change = coeff * (total[0:56] + total[112:168]) + (total[56:112] + total[168:224])
        value = value * (1.0 - change[55:56]) + change
        if kept:
            state[0:56, here] = value
        if later is not None:
            store_parts(later, at - origin, split(value, coeff))

    waiting = None
    for at, width, matrix, kept in places:
        total = matmul(at, width, matrix())
        if waiting is not None:
            finish(*waiting)
        waiting = (at, width, kept, total)
    finish(*waiting)


def interior_blocks(step, count):
    skip = (step + 1) // 2
    return range(skip, count - skip)


def seams(own, side):
    packed = 0
    for step in range(STEPS - 1):
        low = interior_blocks(step, own // BLOCK)[0] * BLOCK
        high = low + REACH + (BLOCK if step % 2 == 0 else 0)
        if side:
            yield step, own - high, own - low, packed
        else:
            yield step, low, high, packed
        packed += high - low


def packed_columns(own):
    return sum(high - low for _, low, high, _ in seams(own, 0))


def interior_kernel(
    head, tail, root, near_adj, far_adj, near_state, far_state, near_parts, far_parts,
    near_values, far_values, near_square, far_square, adj, state, buf0, buf1, buf2, buf3, padded,
):
    bufs = (buf0, buf1, buf2, buf3)
    blocks = adj.shape[0]
    own = blocks * BLOCK
    half = blocks // 2
    for block in range(blocks):
        source, at = (head, block * BLOCK) if block < half else (tail, (block - half) * BLOCK)

        def store(down, across, value):
            spot = (slice(down * LANES, (down + 1) * LANES), slice(across * LANES, (across + 1) * LANES))
            adj[block, *spot] = value
            if block < half:
                near_adj[block, *spot] = value
            if block >= half - 1:
                far_adj[block - (half - 1), *spot] = value

        value = source[:, at : at + BLOCK]
        build_block(value[56:63], store)
        coeff = 0.5 * value[63:64]
        here = block * BLOCK
        state[0:56, here : here + BLOCK] = value[0:56]
        state[56:64, here : here + BLOCK] = jnp.broadcast_to(coeff, (8, BLOCK))
        if block < half - 1:
            near_values[:, here : here + BLOCK] = value[0:56]
        else:
            there = here - (half - 1) * BLOCK
            far_values[:, there : there + BLOCK] = value[0:56]
        store_parts(buf0, here, split(value[0:56], coeff))
    for step in range(1, STEPS - 1):
        whole = interior_blocks(step, blocks)
        places = [(block * BLOCK, BLOCK, functools.partial(lambda b: adj[b], block), True) for block in whole]
        if step % 2:
            low, high = whole[0] - 1, whole[-1] + 1
            places.append((low * BLOCK + REACH, REACH, lambda: adj[low, REACH:, REACH:], False))
            places.append((high * BLOCK, REACH, lambda: adj[high, : BLOCK + REACH, :REACH], False))
        sweep(state, bufs[(step - 1) % 4], bufs[step % 4], (0, 0), places)
    padded[...] = jnp.zeros(padded.shape, jnp.float32)
    padded[0:LEVELS, 0:LEVELS] = root[...]
    matrix = lax.dot_general(
        padded[...], padded[...], (((1,), (1,)), ((), ())),
        precision=lax.Precision.HIGHEST, preferred_element_type=jnp.float32,
    )
    matrix_high = matrix.astype(jnp.bfloat16)
    matrix_low = (matrix - matrix_high.astype(jnp.float32)).astype(jnp.bfloat16)
    near_square[...] = far_square[...] = jnp.concatenate([matrix_high, matrix_low], axis=0)
    near_state[...] = state[:, 0 : own // 2]
    far_state[...] = state[:, own // 2 :]
    for side, parts in ((0, near_parts), (1, far_parts)):
        for step, low, high, packed in seams(own, side):
            parts[:, packed : packed + high - low] = bufs[step % 4][:, low:high]


def load_halo(part, at, state, outer, buf, bases):
    for index in range(HALO // BLOCK):
        value = part[:, index * BLOCK : (index + 1) * BLOCK]
        coeff = 0.5 * value[63:64]
        here = at + index * BLOCK
        spot = slice(here - bases[0], here - bases[0] + BLOCK)
        state[0:56, spot] = value[0:56]
        state[56:64, spot] = jnp.broadcast_to(coeff, (8, BLOCK))
        store_parts(buf, here - bases[1], split(value[0:56], coeff))

        def store(down, across, piece):
            outer[index, down * LANES : (down + 1) * LANES, across * LANES : (across + 1) * LANES] = piece

        build_block(value[56:63], store)


def carry_over(parts, bufs, own, side, bases):
    at = HALO - bases[1]
    for step, low, high, packed in seams(own, side):
        bufs[step % 4][:, at + low : at + high] = parts[:, packed : packed + high - low]


def level_product(square, value):
    high = value.astype(jnp.bfloat16)
    low = (value - high.astype(jnp.float32)).astype(jnp.bfloat16)
    first = jnp.dot(square[...], high, preferred_element_type=jnp.float32)
    second = jnp.dot(square[0:64, :], low, preferred_element_type=jnp.float32)
    return first[0:64] + (first[64:128] + second)


def left_kernel(left, inner, done, parts, values, square, state, seam, outer, buf0, buf1, buf2, buf3):
    own = 2 * done.shape[1]
    bases = (0, -REACH)
    bufs = (buf0, buf1, buf2, buf3)
    fringe = HALO // BLOCK
    middle = fringe + own // BLOCK // 2
    state[:, HALO:] = done[...]
    edge = jnp.zeros((224, REACH), jnp.bfloat16)
    buf0[:, 0:REACH] = edge
    buf2[:, 2 * REACH : 3 * REACH] = edge
    carry_over(parts, bufs, own, 0, bases)
    load_halo(left, 0, state, outer, buf0, bases)
    for step in range(1, STEPS + 1):
        inside = interior_blocks(step, own // BLOCK)
        stop = fringe + inside[0] if len(inside) else middle - (step == STEPS)
        places = [
            (
                block * BLOCK, BLOCK,
                functools.partial(lambda b: outer[b] if b < fringe else inner[b - fringe], block), True,
            )
            for block in range(step // 2, stop)
        ]
        sweep(state, bufs[(step - 1) % 4], bufs[step % 4] if step < STEPS else None, bases, places)
    low = (middle - 1) * BLOCK - REACH - bases[1]
    seam[...] = bufs[(STEPS - 1) % 4][:, low : low + BLOCK + REACH]
    total = jnp.zeros((1, BLOCK), jnp.float32)
    for block in range(own // BLOCK // 2 - 1):
        here = slice(HALO + block * BLOCK, HALO + (block + 1) * BLOCK)
        smoothed = level_product(square, state[:, here])
        state[:, here] = smoothed
        at = block * BLOCK
        total = total + jnp.sum(values[0:LEVELS, at : at + BLOCK] * smoothed[0:LEVELS], axis=0, keepdims=True)
    state[56:57, 0:BLOCK] = total


def right_kernel(
    core, place, right, ens, west, seam, inner, done, parts, values, square,
    keep, send, state, outer, buf0, buf1, buf2, buf3, rowed,
):
    own = 2 * done.shape[1]
    wide = own + 2 * HALO
    tiles = own // LANES
    blocks = wide // BLOCK
    fringe = HALO // BLOCK
    middle = blocks // 2
    bases = ((middle - 1) * BLOCK, (middle - 2) * BLOCK)
    bufs = (buf0, buf1, buf2, buf3)
    state[:, 0:BLOCK] = west[:, (middle - 1) * BLOCK :]
    state[:, BLOCK : BLOCK + own // 2] = done[...]
    edge = jnp.zeros((224, REACH), jnp.bfloat16)
    buf0[:, wide - bases[1] :] = edge
    buf2[:, wide - 2 * REACH - bases[1] : wide - REACH - bases[1]] = edge
    carry_over(parts, bufs, own, 1, bases)
    load_halo(right, HALO + own, state, outer, buf0, bases)
    for step in range(1, STEPS + 1):
        inside = interior_blocks(step, own // BLOCK)
        start = fringe + inside[-1] + 1 if len(inside) else middle - (step == STEPS)
        places = [
            (
                block * BLOCK, BLOCK,
                functools.partial(
                    lambda b: inner[b - (middle - 1)] if b < blocks - fringe else outer[b - (blocks - fringe)], block
                ), True,
            )
            for block in range(start, blocks - step // 2)
        ]
        if step == STEPS:
            low = (middle - 1) * BLOCK - REACH - bases[1]
            bufs[(step - 1) % 4][:, low : low + BLOCK + REACH] = seam[...]
        sweep(state, bufs[(step - 1) % 4], bufs[step % 4] if step < STEPS else None, bases, places)

    total = west[56:57, 0:BLOCK]
    for block in range(own // BLOCK):
        at = (fringe + block) * BLOCK
        if at < bases[0]:
            smoothed = west[0:LEVELS, at : at + BLOCK]
        else:
            smoothed = level_product(square, state[:, at - bases[0] : at - bases[0] + BLOCK])[0:LEVELS]
            there = at - bases[0]
            total = total + jnp.sum(values[0:LEVELS, there : there + BLOCK] * smoothed, axis=0, keepdims=True)
        for tile in range(BLOCK // LANES):
            spot = block * (BLOCK // LANES) + tile
            rowed[pl.ds(spot, LEVELS, stride=tiles), :] = smoothed[:, tile * LANES : (tile + 1) * LANES]
    slots = 4
    chunk = rowed.shape[0] // slots
    spot = pl.ds(slots * chunk, 8)
    keep[spot, :] = send[spot, :] = jnp.broadcast_to(jnp.sum(total, axis=1, keepdims=True), (8, LANES))

    mine, chip = core[0], place[0]
    spare = slots * chunk - LEVELS * tiles

    def products(slot, start, first, count):
        rows = rowed[pl.ds(pl.multiple_of(start + first, 8), count), :]
        at = 2 * (start + first)
        here = pl.ds(slot * chunk + first, count)
        keep[here, :] = ens[pl.ds(at + mine, count, stride=2), :] * rows
        send[here, :] = ens[pl.ds(at + 1 - mine, count, stride=2), :] * rows

    for slot in range(slots):
        target = lax.rem(chip + slot, slots)
        start = target * chunk
        products(slot, start, 0, chunk - spare)

        @pl.when(target < slots - 1)
        def _():
            products(slot, start, chunk - spare, spare)

        @pl.when(target == slots - 1)
        def _():
            nothing = jnp.zeros((spare, LANES), jnp.float32)
            keep[pl.ds((slot + 1) * chunk - spare, spare), :] = nothing
            send[pl.ds((slot + 1) * chunk - spare, spare), :] = nothing


def place_pieces(core, place, slots, same, other, out, lines, sems):
    mine, chip = core[0], place[0]
    chunk = lines.shape[0] // len(slots) // 2
    short = 2 * chunk - (4 * 2 * chunk - out.shape[0])
    waits = []
    for index, slot in enumerate(slots):
        source = lax.rem(chip + 4 - slot, 4)
        start = index * 2 * chunk
        lines[pl.ds(start + mine, chunk, stride=2), :] = same[index, 0:chunk, :]
        lines[pl.ds(start + 1 - mine, chunk, stride=2), :] = other[index, 0:chunk, :]
        target = pl.multiple_of(source * 2 * chunk, 8)
        main = pltpu.make_async_copy(
            lines.at[pl.ds(start, short)], out.at[pl.ds(target, short)], sems.at[0, index]
        )
        extra = pltpu.make_async_copy(
            lines.at[pl.ds(start + short, 2 * chunk - short)],
            out.at[pl.ds(pl.multiple_of(target + short, 8), 2 * chunk - short)],
            sems.at[1, index],
        )
        main.start()
        pl.when(source < 3)(extra.start)
        waits.append((source, main, extra))
    return waits


def wait_pieces(waits):
    for source, main, extra in waits:
        main.wait()
        pl.when(source < 3)(extra.wait)


def early_kernel(core, place, same, other, out, lines, sems):
    wait_pieces(place_pieces(core, place, EARLY, same, other, out, lines, sems))


def late_kernel(scale, core, place, begun, early, same, other, out, quadratic, lines, sems):
    waits = place_pieces(core, place, LATE, same, other, out, lines, sems)
    chunk = lines.shape[0] // len(LATE) // 2
    near, far = [
        pieces[0, chunk : chunk + 8, :] + pieces[1, chunk : chunk + 8, :] for pieces in (early, same)
    ]
    quadratic[0, 0] = jnp.max(near + far) * scale
    wait_pieces(waits)


def interleave(array):
    cells = array.shape[2]
    array = array.reshape(2, LEVELS, cells // LANES, LANES)
    return array.transpose(1, 2, 0, 3).reshape(-1, LANES)


def on_device(ensemble, field, diffusivity, neighbours, vertical_root):
    own = diffusivity.shape[0]
    patches = lax.axis_size("patch")
    members = lax.axis_size("mem")
    chips = members // 2
    all_cells = own * patches
    half = own // 2
    tiles = own // LANES
    vmem = pl.BlockSpec(memory_space=pltpu.VMEM)
    smem = pl.BlockSpec(memory_space=pltpu.SMEM)
    hbm = pl.BlockSpec(memory_space=pltpu.HBM)
    params = pltpu.CompilerParams(vmem_limit_bytes=32 * 1024 * 1024)
    place = (lax.axis_index("patch") * own).astype(jnp.int32).reshape(1)
    member = lax.axis_index("mem")
    ids = [
        jnp.bitwise_and(member, 1).astype(jnp.int32).reshape(1),
        lax.shift_right_logical(member, 1).astype(jnp.int32).reshape(1),
    ]
    ens_rows = interleave(ensemble[0])
    field_rows = interleave(field)

    in_hbm = [
        pltpu.with_memory_space_constraint(array, pltpu.HBM)
        for array in (ens_rows, field_rows, diffusivity.reshape(1, own), neighbours)
    ]
    side = jax.ShapeDtypeStruct((64, half), jnp.float32)
    head, tail = pl.pallas_call(
        functools.partial(prepare_kernel, all_cells),
        out_shape=(side, side),
        in_specs=[smem, hbm, hbm, hbm, hbm],
        out_specs=(vmem, vmem),
        scratch_shapes=[
            pltpu.VMEM(ens_rows.shape, jnp.float32),
            pltpu.VMEM(ens_rows.shape, jnp.float32),
            pltpu.VMEM((1, own), jnp.float32),
            pltpu.VMEM((7, own), jnp.int32),
            pltpu.SemaphoreType.DMA((3, 4)),
        ],
        compiler_params=params,
        name="prepare",
    )(place, *in_hbm)

    left = lax.ppermute(tail, "patch", [(i, (i + 1) % patches) for i in range(patches)])
    right = lax.ppermute(head, "patch", [((i + 1) % patches, i) for i in range(patches)])

    blocks = own // BLOCK
    adjacency = (2 * BLOCK, BLOCK)
    packed = jax.ShapeDtypeStruct((224, packed_columns(own)), jnp.bfloat16)
    half_state = jax.ShapeDtypeStruct((64, half), jnp.float32)
    squared = jax.ShapeDtypeStruct((128, 64), jnp.bfloat16)
    inside = pl.pallas_call(
        interior_kernel,
        out_shape=(
            jax.ShapeDtypeStruct((blocks // 2, *adjacency), jnp.bfloat16),
            jax.ShapeDtypeStruct((blocks // 2 + 1, *adjacency), jnp.bfloat16),
            half_state, half_state, packed, packed,
            jax.ShapeDtypeStruct((56, half - BLOCK), jnp.float32),
            jax.ShapeDtypeStruct((56, half + BLOCK), jnp.float32),
            squared, squared,
        ),
        in_specs=[vmem] * 3,
        out_specs=(vmem,) * 10,
        scratch_shapes=[pltpu.VMEM((blocks, *adjacency), jnp.bfloat16), pltpu.VMEM((64, own), jnp.float32)]
        + [pltpu.VMEM((224, own), jnp.bfloat16)] * 4
        + [pltpu.VMEM((64, 64), jnp.float32)],
        compiler_params=params,
        cost_estimate=pl.CostEstimate(flops=4_000_000_000, bytes_accessed=4_000_000, transcendentals=0),
        name="interior",
    )(head, tail, vertical_root)

    chunk = 56 * tiles // chips
    west, seam = pl.pallas_call(
        left_kernel,
        out_shape=(
            jax.ShapeDtypeStruct((64, HALO + half), jnp.float32),
            jax.ShapeDtypeStruct((224, BLOCK + REACH), jnp.bfloat16),
        ),
        in_specs=[vmem] * 6,
        out_specs=(vmem,) * 2,
        scratch_shapes=[pltpu.VMEM((HALO // BLOCK, 2 * BLOCK, BLOCK), jnp.bfloat16)]
        + [pltpu.VMEM((224, HALO + half + 2 * REACH), jnp.bfloat16)] * 4,
        compiler_params=params,
        cost_estimate=pl.CostEstimate(flops=0, bytes_accessed=7_000_000, transcendentals=0),
        name="left",
    )(left, *inside[0::2])
    terms = jax.ShapeDtypeStruct((chips * chunk + 8, LANES), jnp.float32)
    keep, send = pl.pallas_call(
        right_kernel,
        out_shape=(terms, terms),
        in_specs=[smem] * 2 + [vmem] * 9,
        out_specs=(vmem, vmem),
        scratch_shapes=[
            pltpu.VMEM((64, BLOCK + half + HALO), jnp.float32),
            pltpu.VMEM((HALO // BLOCK, 2 * BLOCK, BLOCK), jnp.bfloat16),
        ]
        + [pltpu.VMEM((224, 2 * BLOCK + half + HALO + REACH), jnp.bfloat16)] * 4
        + [pltpu.VMEM((56 * tiles, LANES), jnp.float32)],
        compiler_params=params,
        cost_estimate=pl.CostEstimate(flops=0, bytes_accessed=7_000_000, transcendentals=0),
        name="right",
    )(*ids, right, ens_rows, west, seam, *inside[1::2])

    def shift_chips(array, by):
        pairs = [(2 * z + c, 2 * ((z + by) % chips) + c) for z in range(chips) for c in range(2)]
        return lax.ppermute(array, "mem", pairs)

    twin = [(i, i ^ 1) for i in range(members)]
    order = [2, 1, 3]
    pair_sum = keep + lax.ppermute(send, "mem", twin)
    pieces = [pair_sum[chunk * slot : chunk * (slot + 1)] for slot in range(chips)]
    terms = {by: shift_chips(pieces[by], by) for by in order}
    spread = jnp.broadcast_to(pair_sum[chips * chunk : chips * chunk + 1][None], (patches, 1, LANES))
    spread = lax.all_to_all(spread, "patch", 0, 0)
    terms, spread = lax.optimization_barrier((terms, spread))
    total = (pieces[0] + terms[1] + terms[2] + terms[3]) / (members - 1.0)
    total = jnp.concatenate([total, jnp.broadcast_to(jnp.sum(spread, axis=0), (8, LANES))], axis=0)
    copies = {by: shift_chips(total, by) for by in order}
    sources = {0: total, **copies}
    scale = 1.0 / ((members - 1.0) * field.shape[0] * field.shape[1] * all_cells)
    scratch = [
        pltpu.VMEM((2 * chunk * 2, LANES), jnp.float32),
        pltpu.SemaphoreType.DMA((2, 2)),
    ]
    early = jnp.stack([sources[by] for by in EARLY])
    rows = pl.pallas_call(
        early_kernel,
        out_shape=jax.ShapeDtypeStruct(field_rows.shape, jnp.float32),
        in_specs=[smem, smem, vmem, vmem],
        out_specs=hbm,
        scratch_shapes=scratch,
        compiler_params=params,
        cost_estimate=pl.CostEstimate(flops=1_000_000, bytes_accessed=4_000_000, transcendentals=0),
        name="early",
    )(*ids, early, lax.ppermute(early, "mem", twin))
    late = jnp.stack([sources[by] for by in LATE])
    rows, quadratic = pl.pallas_call(
        functools.partial(late_kernel, scale),
        out_shape=(
            jax.ShapeDtypeStruct(field_rows.shape, jnp.float32),
            jax.ShapeDtypeStruct((1, 1), jnp.float32),
        ),
        in_specs=[smem, smem, hbm, vmem, vmem, vmem],
        out_specs=(hbm, smem),
        scratch_shapes=scratch,
        input_output_aliases={2: 0},
        compiler_params=params,
        name="late",
    )(*ids, rows, early, late, lax.ppermute(late, "mem", twin))
    product = rows.reshape(LEVELS, tiles, 2, LANES).transpose(2, 0, 1, 3).reshape(field.shape)
    return (product, quadratic.reshape(()))


def solution(mesh):
    return jax.shard_map(
        on_device,
        mesh=mesh,
        in_specs=(
            P("mem", None, None, "patch"),
            P(None, None, "patch"),
            P("patch"),
            P(None, "patch"),
            P(),
        ),
        out_specs=(P(None, None, "patch"), P()),
        check_vma=False,
    )
```

```python
import functools

import jax
import jax.numpy as jnp
from jax import lax
from jax.experimental import pallas as pl
from jax.experimental.pallas import tpu as pltpu
from jax.sharding import PartitionSpec as P

STEPS = 8
REACH = 128
BLOCK = 256
HALO = STEPS * REACH
LEVELS = 55
LANES = 128
EARLY, LATE = (0, 2), (1, 3)


def prepare_kernel(
    all_cells, place, ens, field, diff, neigh, head, tail, ens_in, field_in, diff_in, neigh_in, sems
):
    own = diff.shape[1]
    tiles = own // LANES
    half = own // 2
    start = place[0]
    levels = (0, 16, 32, 48, LEVELS)
    copies = []
    for turn in range(4):
        rows = pl.ds(levels[turn] * 2 * tiles, (levels[turn + 1] - levels[turn]) * 2 * tiles)
        copies.append((
            pltpu.make_async_copy(ens.at[rows], ens_in.at[rows], sems.at[0, turn]),
            pltpu.make_async_copy(field.at[rows], field_in.at[rows], sems.at[1, turn]),
        ))
    others = (
        pltpu.make_async_copy(neigh, neigh_in, sems.at[2, 0]),
        pltpu.make_async_copy(diff, diff_in, sems.at[2, 1]),
    )
    for copy in others + copies[0] + copies[1] + copies[2] + copies[3]:
        copy.start()
    for copy in others:
        copy.wait()
    for part, out in ((0, head), (1, tail)):
        cols = pl.ds(part * half, half)
        out[55:56, :] = jnp.ones((1, half), jnp.float32)
        cell = lax.broadcasted_iota(jnp.int32, (7, half), 1) + (start + part * half)
        shift = neigh_in[:, cols] - cell
        shift = jnp.where(shift > all_cells // 2, shift - all_cells, shift)
        shift = jnp.where(shift < -(all_cells // 2), shift + all_cells, shift)
        out[56:63, :] = shift.astype(jnp.float32)
        out[63:64, :] = diff_in[:, cols]
    for turn in range(4):
        for copy in copies[turn]:
            copy.wait()
        low, high = levels[turn], levels[turn + 1]
        rows = pl.ds(low * 2 * tiles, (high - low) * 2 * tiles)
        ens_in[rows, :] = ens_in[rows, :] * field_in[rows, :]
        for part, out in ((0, head), (1, tail)):
            for tile in range(tiles // 2):
                at = low * 2 * tiles + 2 * (part * (tiles // 2) + tile)
                out[low:high, tile * LANES : (tile + 1) * LANES] = (
                    ens_in[pl.ds(at, high - low, stride=2 * tiles), :]
                    + ens_in[pl.ds(at + 1, high - low, stride=2 * tiles), :]
                )


def build_block(shift, store):
    row = lax.broadcasted_iota(jnp.int32, (LANES, LANES), 0).astype(jnp.float32).astype(jnp.bfloat16)
    lane = lax.broadcasted_iota(jnp.int32, (1, LANES), 1).astype(jnp.float32)
    one = jnp.ones((LANES, LANES), jnp.bfloat16)
    zero = jnp.zeros((LANES, LANES), jnp.bfloat16)
    for chunk in range(BLOCK // LANES):
        part = shift[:, chunk * LANES : (chunk + 1) * LANES]
        for side in range(3):
            local = part + (lane + (1.0 - side) * LANES)
            inside = jnp.logical_and(jnp.logical_and(local >= 0.0, local < LANES), part != 0.0)
            local = jnp.where(inside, local, -1.0).astype(jnp.bfloat16)
            hit = zero
            for slot in range(7):
                hit = jnp.where(row == local[slot : slot + 1, :], one, hit)
            store(chunk + side, chunk, hit)
        store((chunk + 3) % 4, chunk, zero)


def split(value, coeff):
    both = jnp.concatenate([value, coeff * value], axis=0)
    high = both.astype(jnp.bfloat16)
    low = (both - high.astype(jnp.float32)).astype(jnp.bfloat16)
    return high, low


def store_parts(buf, at, parts):
    width = parts[0].shape[1]
    buf[0:112, at : at + width] = parts[0]
    buf[112:224, at : at + width] = parts[1]


def sweep(state, now, later, bases, places):
    first, origin = bases

    def matmul(at, width, matrix):
        low = at - origin - REACH
        return jnp.dot(now[:, low : low + width + 2 * REACH], matrix, preferred_element_type=jnp.float32)

    def finish(at, width, kept, total):
        here = slice(at - first, at - first + width)
        coeff = state[56:57, here]
        value = state[0:56, here]
        change = coeff * (total[0:56] + total[112:168]) + (total[56:112] + total[168:224])
        value = value * (1.0 - change[55:56]) + change
        if kept:
            state[0:56, here] = value
        if later is not None:
            store_parts(later, at - origin, split(value, coeff))

    waiting = None
    for at, width, matrix, kept in places:
        total = matmul(at, width, matrix())
        if waiting is not None:
            finish(*waiting)
        waiting = (at, width, kept, total)
    finish(*waiting)


def interior_blocks(step, count):
    skip = (step + 1) // 2
    return range(skip, count - skip)


def seams(own, side):
    packed = 0
    for step in range(STEPS - 1):
        low = interior_blocks(step, own // BLOCK)[0] * BLOCK
        high = low + REACH + (BLOCK if step % 2 == 0 else 0)
        if side:
            yield step, own - high, own - low, packed
        else:
            yield step, low, high, packed
        packed += high - low


def packed_columns(own):
    return sum(high - low for _, low, high, _ in seams(own, 0))


def interior_kernel(
    head, tail, root, near_adj, far_adj, near_state, far_state, near_parts, far_parts,
    near_values, far_values, near_square, far_square, adj, state, buf0, buf1, buf2, buf3, padded,
):
    bufs = (buf0, buf1, buf2, buf3)
    blocks = adj.shape[0]
    own = blocks * BLOCK
    half = blocks // 2
    for block in range(blocks):
        source, at = (head, block * BLOCK) if block < half else (tail, (block - half) * BLOCK)

        def store(down, across, value):
            spot = (slice(down * LANES, (down + 1) * LANES), slice(across * LANES, (across + 1) * LANES))
            adj[block, *spot] = value
            if block < half:
                near_adj[block, *spot] = value
            if block >= half - 1:
                far_adj[block - (half - 1), *spot] = value

        value = source[:, at : at + BLOCK]
        build_block(value[56:63], store)
        coeff = 0.5 * value[63:64]
        here = block * BLOCK
        state[0:56, here : here + BLOCK] = value[0:56]
        state[56:64, here : here + BLOCK] = jnp.broadcast_to(coeff, (8, BLOCK))
        if block < half - 1:
            near_values[:, here : here + BLOCK] = value[0:56]
        else:
            there = here - (half - 1) * BLOCK
            far_values[:, there : there + BLOCK] = value[0:56]
        store_parts(buf0, here, split(value[0:56], coeff))
    for step in range(1, STEPS - 1):
        whole = interior_blocks(step, blocks)
        places = [(block * BLOCK, BLOCK, functools.partial(lambda b: adj[b], block), True) for block in whole]
        if step % 2:
            low, high = whole[0] - 1, whole[-1] + 1
            places.append((low * BLOCK + REACH, REACH, lambda: adj[low, REACH:, REACH:], False))
            places.append((high * BLOCK, REACH, lambda: adj[high, : BLOCK + REACH, :REACH], False))
        sweep(state, bufs[(step - 1) % 4], bufs[step % 4], (0, 0), places)
    padded[...] = jnp.zeros(padded.shape, jnp.float32)
    padded[0:LEVELS, 0:LEVELS] = root[...]
    matrix = lax.dot_general(
        padded[...], padded[...], (((1,), (1,)), ((), ())),
        precision=lax.Precision.HIGHEST, preferred_element_type=jnp.float32,
    )
    matrix_high = matrix.astype(jnp.bfloat16)
    matrix_low = (matrix - matrix_high.astype(jnp.float32)).astype(jnp.bfloat16)
    near_square[...] = far_square[...] = jnp.concatenate([matrix_high, matrix_low], axis=0)
    near_state[...] = state[:, 0 : own // 2]
    far_state[...] = state[:, own // 2 :]
    for side, parts in ((0, near_parts), (1, far_parts)):
        for step, low, high, packed in seams(own, side):
            parts[:, packed : packed + high - low] = bufs[step % 4][:, low:high]


def load_halo(part, at, state, outer, buf, bases):
    for index in range(HALO // BLOCK):
        value = part[:, index * BLOCK : (index + 1) * BLOCK]
        coeff = 0.5 * value[63:64]
        here = at + index * BLOCK
        spot = slice(here - bases[0], here - bases[0] + BLOCK)
        state[0:56, spot] = value[0:56]
        state[56:64, spot] = jnp.broadcast_to(coeff, (8, BLOCK))
        store_parts(buf, here - bases[1], split(value[0:56], coeff))

        def store(down, across, piece):
            outer[index, down * LANES : (down + 1) * LANES, across * LANES : (across + 1) * LANES] = piece

        build_block(value[56:63], store)


def carry_over(parts, bufs, own, side, bases):
    at = HALO - bases[1]
    for step, low, high, packed in seams(own, side):
        bufs[step % 4][:, at + low : at + high] = parts[:, packed : packed + high - low]


def level_product(square, value):
    high = value.astype(jnp.bfloat16)
    low = (value - high.astype(jnp.float32)).astype(jnp.bfloat16)
    first = jnp.dot(square[...], high, preferred_element_type=jnp.float32)
    second = jnp.dot(square[0:64, :], low, preferred_element_type=jnp.float32)
    return first[0:64] + (first[64:128] + second)


def left_kernel(left, inner, done, parts, values, square, state, seam, outer, buf0, buf1, buf2, buf3):
    own = 2 * done.shape[1]
    bases = (0, -REACH)
    bufs = (buf0, buf1, buf2, buf3)
    fringe = HALO // BLOCK
    middle = fringe + own // BLOCK // 2
    state[:, HALO:] = done[...]
    edge = jnp.zeros((224, REACH), jnp.bfloat16)
    buf0[:, 0:REACH] = edge
    buf2[:, 2 * REACH : 3 * REACH] = edge
    carry_over(parts, bufs, own, 0, bases)
    load_halo(left, 0, state, outer, buf0, bases)
    for step in range(1, STEPS + 1):
        inside = interior_blocks(step, own // BLOCK)
        stop = fringe + inside[0] if len(inside) else middle - (step == STEPS)
        places = [
            (
                block * BLOCK, BLOCK,
                functools.partial(lambda b: outer[b] if b < fringe else inner[b - fringe], block), True,
            )
            for block in range(step // 2, stop)
        ]
        sweep(state, bufs[(step - 1) % 4], bufs[step % 4] if step < STEPS else None, bases, places)
    low = (middle - 1) * BLOCK - REACH - bases[1]
    seam[...] = bufs[(STEPS - 1) % 4][:, low : low + BLOCK + REACH]
    total = jnp.zeros((1, BLOCK), jnp.float32)
    for block in range(own // BLOCK // 2 - 1):
        here = slice(HALO + block * BLOCK, HALO + (block + 1) * BLOCK)
        smoothed = level_product(square, state[:, here])
        state[:, here] = smoothed
        at = block * BLOCK
        total = total + jnp.sum(values[0:LEVELS, at : at + BLOCK] * smoothed[0:LEVELS], axis=0, keepdims=True)
    state[56:57, 0:BLOCK] = total


def right_kernel(
    core, place, right, ens, west, seam, inner, done, parts, values, square,
    keep, send, state, outer, buf0, buf1, buf2, buf3, rowed,
):
    own = 2 * done.shape[1]
    wide = own + 2 * HALO
    tiles = own // LANES
    blocks = wide // BLOCK
    fringe = HALO // BLOCK
    middle = blocks // 2
    bases = ((middle - 1) * BLOCK, (middle - 2) * BLOCK)
    bufs = (buf0, buf1, buf2, buf3)
    state[:, 0:BLOCK] = west[:, (middle - 1) * BLOCK :]
    state[:, BLOCK : BLOCK + own // 2] = done[...]
    edge = jnp.zeros((224, REACH), jnp.bfloat16)
    buf0[:, wide - bases[1] :] = edge
    buf2[:, wide - 2 * REACH - bases[1] : wide - REACH - bases[1]] = edge
    carry_over(parts, bufs, own, 1, bases)
    load_halo(right, HALO + own, state, outer, buf0, bases)
    for step in range(1, STEPS + 1):
        inside = interior_blocks(step, own // BLOCK)
        start = fringe + inside[-1] + 1 if len(inside) else middle - (step == STEPS)
        places = [
            (
                block * BLOCK, BLOCK,
                functools.partial(
                    lambda b: inner[b - (middle - 1)] if b < blocks - fringe else outer[b - (blocks - fringe)], block
                ), True,
            )
            for block in range(start, blocks - step // 2)
        ]
        if step == STEPS:
            low = (middle - 1) * BLOCK - REACH - bases[1]
            bufs[(step - 1) % 4][:, low : low + BLOCK + REACH] = seam[...]
        sweep(state, bufs[(step - 1) % 4], bufs[step % 4] if step < STEPS else None, bases, places)

    total = west[56:57, 0:BLOCK]
    for block in range(own // BLOCK):
        at = (fringe + block) * BLOCK
        if at < bases[0]:
            smoothed = west[0:LEVELS, at : at + BLOCK]
        else:
            smoothed = level_product(square, state[:, at - bases[0] : at - bases[0] + BLOCK])[0:LEVELS]
            there = at - bases[0]
            total = total + jnp.sum(values[0:LEVELS, there : there + BLOCK] * smoothed, axis=0, keepdims=True)
        for tile in range(BLOCK // LANES):
            spot = block * (BLOCK // LANES) + tile
            rowed[pl.ds(spot, LEVELS, stride=tiles), :] = smoothed[:, tile * LANES : (tile + 1) * LANES]
    slots = 4
    chunk = rowed.shape[0] // slots
    spot = pl.ds(slots * chunk, 8)
    keep[spot, :] = send[spot, :] = jnp.broadcast_to(jnp.sum(total, axis=1, keepdims=True), (8, LANES))

    mine, chip = core[0], place[0]
    spare = slots * chunk - LEVELS * tiles

    def products(slot, start, first, count):
        rows = rowed[pl.ds(pl.multiple_of(start + first, 8), count), :]
        at = 2 * (start + first)
        here = pl.ds(slot * chunk + first, count)
        keep[here, :] = ens[pl.ds(at + mine, count, stride=2), :] * rows
        send[here, :] = ens[pl.ds(at + 1 - mine, count, stride=2), :] * rows

    for slot in range(slots):
        target = lax.rem(chip + slot, slots)
        start = target * chunk
        products(slot, start, 0, chunk - spare)

        @pl.when(target < slots - 1)
        def _():
            products(slot, start, chunk - spare, spare)

        @pl.when(target == slots - 1)
        def _():
            nothing = jnp.zeros((spare, LANES), jnp.float32)
            keep[pl.ds((slot + 1) * chunk - spare, spare), :] = nothing
            send[pl.ds((slot + 1) * chunk - spare, spare), :] = nothing


def place_pieces(core, place, slots, same, other, out, lines, sems):
    mine, chip = core[0], place[0]
    chunk = lines.shape[0] // len(slots) // 2
    short = 2 * chunk - (4 * 2 * chunk - out.shape[0])
    waits = []
    for index, slot in enumerate(slots):
        source = lax.rem(chip + 4 - slot, 4)
        start = index * 2 * chunk
        lines[pl.ds(start + mine, chunk, stride=2), :] = same[index, 0:chunk, :]
        lines[pl.ds(start + 1 - mine, chunk, stride=2), :] = other[index, 0:chunk, :]
        target = pl.multiple_of(source * 2 * chunk, 8)
        main = pltpu.make_async_copy(
            lines.at[pl.ds(start, short)], out.at[pl.ds(target, short)], sems.at[0, index]
        )
        extra = pltpu.make_async_copy(
            lines.at[pl.ds(start + short, 2 * chunk - short)],
            out.at[pl.ds(pl.multiple_of(target + short, 8), 2 * chunk - short)],
            sems.at[1, index],
        )
        main.start()
        pl.when(source < 3)(extra.start)
        waits.append((source, main, extra))
    return waits


def wait_pieces(waits):
    for source, main, extra in waits:
        main.wait()
        pl.when(source < 3)(extra.wait)


def early_kernel(scale, core, place, same, other, late, out, quadratic, lines, sems):
    waits = place_pieces(core, place, EARLY, same, other, out, lines, sems)
    chunk = lines.shape[0] // len(EARLY) // 2
    near, far = [
        pieces[0, chunk : chunk + 8, :] + pieces[1, chunk : chunk + 8, :] for pieces in (same, late)
    ]
    quadratic[0, 0] = jnp.max(near + far) * scale
    wait_pieces(waits)


def late_kernel(core, place, begun, same, other, out, lines, sems):
    wait_pieces(place_pieces(core, place, LATE, same, other, out, lines, sems))


def interleave(array):
    cells = array.shape[2]
    array = array.reshape(2, LEVELS, cells // LANES, LANES)
    return array.transpose(1, 2, 0, 3).reshape(-1, LANES)


def on_device(ensemble, field, diffusivity, neighbours, vertical_root):
    own = diffusivity.shape[0]
    patches = lax.axis_size("patch")
    members = lax.axis_size("mem")
    chips = members // 2
    all_cells = own * patches
    half = own // 2
    tiles = own // LANES
    vmem = pl.BlockSpec(memory_space=pltpu.VMEM)
    smem = pl.BlockSpec(memory_space=pltpu.SMEM)
    hbm = pl.BlockSpec(memory_space=pltpu.HBM)
    params = pltpu.CompilerParams(vmem_limit_bytes=32 * 1024 * 1024)
    place = (lax.axis_index("patch") * own).astype(jnp.int32).reshape(1)
    member = lax.axis_index("mem")
    ids = [
        jnp.bitwise_and(member, 1).astype(jnp.int32).reshape(1),
        lax.shift_right_logical(member, 1).astype(jnp.int32).reshape(1),
    ]
    ens_rows = interleave(ensemble[0])
    field_rows = interleave(field)

    in_hbm = [
        pltpu.with_memory_space_constraint(array, pltpu.HBM)
        for array in (ens_rows, field_rows, diffusivity.reshape(1, own), neighbours)
    ]
    side = jax.ShapeDtypeStruct((64, half), jnp.float32)
    head, tail = pl.pallas_call(
        functools.partial(prepare_kernel, all_cells),
        out_shape=(side, side),
        in_specs=[smem, hbm, hbm, hbm, hbm],
        out_specs=(vmem, vmem),
        scratch_shapes=[
            pltpu.VMEM(ens_rows.shape, jnp.float32),
            pltpu.VMEM(ens_rows.shape, jnp.float32),
            pltpu.VMEM((1, own), jnp.float32),
            pltpu.VMEM((7, own), jnp.int32),
            pltpu.SemaphoreType.DMA((3, 4)),
        ],
        compiler_params=params,
        name="prepare",
    )(place, *in_hbm)

    left = lax.ppermute(tail, "patch", [(i, (i + 1) % patches) for i in range(patches)])
    right = lax.ppermute(head, "patch", [((i + 1) % patches, i) for i in range(patches)])

    blocks = own // BLOCK
    adjacency = (2 * BLOCK, BLOCK)
    packed = jax.ShapeDtypeStruct((224, packed_columns(own)), jnp.bfloat16)
    half_state = jax.ShapeDtypeStruct((64, half), jnp.float32)
    squared = jax.ShapeDtypeStruct((128, 64), jnp.bfloat16)
    inside = pl.pallas_call(
        interior_kernel,
        out_shape=(
            jax.ShapeDtypeStruct((blocks // 2, *adjacency), jnp.bfloat16),
            jax.ShapeDtypeStruct((blocks // 2 + 1, *adjacency), jnp.bfloat16),
            half_state, half_state, packed, packed,
            jax.ShapeDtypeStruct((56, half - BLOCK), jnp.float32),
            jax.ShapeDtypeStruct((56, half + BLOCK), jnp.float32),
            squared, squared,
        ),
        in_specs=[vmem] * 3,
        out_specs=(vmem,) * 10,
        scratch_shapes=[pltpu.VMEM((blocks, *adjacency), jnp.bfloat16), pltpu.VMEM((64, own), jnp.float32)]
        + [pltpu.VMEM((224, own), jnp.bfloat16)] * 4
        + [pltpu.VMEM((64, 64), jnp.float32)],
        compiler_params=params,
        cost_estimate=pl.CostEstimate(flops=4_000_000_000, bytes_accessed=4_000_000, transcendentals=0),
        name="interior",
    )(head, tail, vertical_root)

    chunk = 56 * tiles // chips
    west, seam = pl.pallas_call(
        left_kernel,
        out_shape=(
            jax.ShapeDtypeStruct((64, HALO + half), jnp.float32),
            jax.ShapeDtypeStruct((224, BLOCK + REACH), jnp.bfloat16),
        ),
        in_specs=[vmem] * 6,
        out_specs=(vmem,) * 2,
        scratch_shapes=[pltpu.VMEM((HALO // BLOCK, 2 * BLOCK, BLOCK), jnp.bfloat16)]
        + [pltpu.VMEM((224, HALO + half + 2 * REACH), jnp.bfloat16)] * 4,
        compiler_params=params,
        cost_estimate=pl.CostEstimate(flops=0, bytes_accessed=7_000_000, transcendentals=0),
        name="left",
    )(left, *inside[0::2])
    terms = jax.ShapeDtypeStruct((chips * chunk + 8, LANES), jnp.float32)
    keep, send = pl.pallas_call(
        right_kernel,
        out_shape=(terms, terms),
        in_specs=[smem] * 2 + [vmem] * 9,
        out_specs=(vmem, vmem),
        scratch_shapes=[
            pltpu.VMEM((64, BLOCK + half + HALO), jnp.float32),
            pltpu.VMEM((HALO // BLOCK, 2 * BLOCK, BLOCK), jnp.bfloat16),
        ]
        + [pltpu.VMEM((224, 2 * BLOCK + half + HALO + REACH), jnp.bfloat16)] * 4
        + [pltpu.VMEM((56 * tiles, LANES), jnp.float32)],
        compiler_params=params,
        cost_estimate=pl.CostEstimate(flops=0, bytes_accessed=7_000_000, transcendentals=0),
        name="right",
    )(*ids, right, ens_rows, west, seam, *inside[1::2])

    def shift_chips(array, by):
        pairs = [(2 * z + c, 2 * ((z + by) % chips) + c) for z in range(chips) for c in range(2)]
        return lax.ppermute(array, "mem", pairs)

    twin = [(i, i ^ 1) for i in range(members)]
    order = [2, 1, 3]
    pair_sum = keep + lax.ppermute(send, "mem", twin)
    pieces = [pair_sum[chunk * slot : chunk * (slot + 1)] for slot in range(chips)]
    terms = {by: shift_chips(pieces[by], by) for by in order}
    spread = jnp.broadcast_to(pair_sum[chips * chunk : chips * chunk + 1][None], (patches, 1, LANES))
    spread = lax.all_to_all(spread, "patch", 0, 0)
    terms, spread = lax.optimization_barrier((terms, spread))
    total = (pieces[0] + terms[1] + terms[2] + terms[3]) / (members - 1.0)
    total = jnp.concatenate([total, jnp.broadcast_to(jnp.sum(spread, axis=0), (8, LANES))], axis=0)
    copies = {by: shift_chips(total, by) for by in order}
    sources = {0: total, **copies}
    scale = 1.0 / ((members - 1.0) * field.shape[0] * field.shape[1] * all_cells)
    scratch = [
        pltpu.VMEM((2 * chunk * 2, LANES), jnp.float32),
        pltpu.SemaphoreType.DMA((2, 2)),
    ]
    early = jnp.stack([sources[by] for by in EARLY])
    late = jnp.stack([sources[by] for by in LATE])
    rows, quadratic = pl.pallas_call(
        functools.partial(early_kernel, scale),
        out_shape=(
            jax.ShapeDtypeStruct(field_rows.shape, jnp.float32),
            jax.ShapeDtypeStruct((1, 1), jnp.float32),
        ),
        in_specs=[smem, smem, vmem, vmem, vmem],
        out_specs=(hbm, smem),
        scratch_shapes=scratch,
        compiler_params=params,
        cost_estimate=pl.CostEstimate(flops=1_000_000, bytes_accessed=4_000_000, transcendentals=0),
        name="early",
    )(*ids, early, lax.ppermute(early, "mem", twin), late)
    rows = pl.pallas_call(
        late_kernel,
        out_shape=jax.ShapeDtypeStruct(field_rows.shape, jnp.float32),
        in_specs=[smem, smem, hbm, vmem, vmem],
        out_specs=hbm,
        scratch_shapes=scratch,
        input_output_aliases={2: 0},
        compiler_params=params,
        name="late",
    )(*ids, rows, late, lax.ppermute(late, "mem", twin))
    product = rows.reshape(LEVELS, tiles, 2, LANES).transpose(2, 0, 1, 3).reshape(field.shape)
    return (product, quadratic.reshape(()))


def solution(mesh):
    return jax.shard_map(
        on_device,
        mesh=mesh,
        in_specs=(
            P("mem", None, None, "patch"),
            P(None, None, "patch"),
            P("patch"),
            P(None, "patch"),
            P(),
        ),
        out_specs=(P(None, None, "patch"), P()),
        check_vma=False,
    )
```

```python
import functools

import jax
import jax.numpy as jnp
from jax import lax
from jax.experimental import pallas as pl
from jax.experimental.pallas import tpu as pltpu
from jax.sharding import PartitionSpec as P

STEPS = 8
REACH = 128
BLOCK = 256
HALO = STEPS * REACH
LEVELS = 55
LANES = 128
EARLY, LATE = (0, 2), (1, 3)


def prepare_kernel(
    all_cells, part, place, ens, field, diff, neigh, out, ens_in, field_in, diff_in, neigh_in, sems
):
    tiles = ens.shape[1] // 2
    half = diff.shape[1] // 2
    cols = pl.ds(part * half, half)
    levels = (0, 16, 32, 48, LEVELS)
    copies = []
    for turn in range(4):
        rows = pl.ds(levels[turn], levels[turn + 1] - levels[turn])
        copies.append(tuple(
            pltpu.make_async_copy(
                source.at[rows, pl.ds(part * tiles, tiles)], target.at[rows], sems.at[which, turn]
            )
            for which, (source, target) in enumerate(((ens, ens_in), (field, field_in)))
        ))
    others = (
        pltpu.make_async_copy(neigh.at[:, cols], neigh_in, sems.at[2, 0]),
        pltpu.make_async_copy(diff.at[:, cols], diff_in, sems.at[2, 1]),
    )
    for copy in others + copies[0] + copies[1] + copies[2] + copies[3]:
        copy.start()
    for copy in others:
        copy.wait()
    out[55:56, :] = jnp.ones((1, half), jnp.float32)
    cell = lax.broadcasted_iota(jnp.int32, (7, half), 1) + (place[0] + part * half)
    shift = neigh_in[...] - cell
    shift = jnp.where(shift > all_cells // 2, shift - all_cells, shift)
    shift = jnp.where(shift < -(all_cells // 2), shift + all_cells, shift)
    out[56:63, :] = shift.astype(jnp.float32)
    out[63:64, :] = diff_in[...]
    ens_flat = ens_in.reshape(LEVELS * tiles, LANES)
    field_flat = field_in.reshape(LEVELS * tiles, LANES)
    for turn in range(4):
        for copy in copies[turn]:
            copy.wait()
        low, high = levels[turn], levels[turn + 1]
        rows = pl.ds(low * tiles, (high - low) * tiles)
        ens_flat[rows, :] = ens_flat[rows, :] * field_flat[rows, :]
        for tile in range(tiles // 2):
            at = low * tiles + 2 * tile
            out[low:high, tile * LANES : (tile + 1) * LANES] = (
                ens_flat[pl.ds(at, high - low, stride=tiles), :]
                + ens_flat[pl.ds(at + 1, high - low, stride=tiles), :]
            )


def build_block(shift, store):
    row = lax.broadcasted_iota(jnp.int32, (LANES, LANES), 0).astype(jnp.float32).astype(jnp.bfloat16)
    lane = lax.broadcasted_iota(jnp.int32, (1, LANES), 1).astype(jnp.float32)
    one = jnp.ones((LANES, LANES), jnp.bfloat16)
    zero = jnp.zeros((LANES, LANES), jnp.bfloat16)
    for chunk in range(BLOCK // LANES):
        part = shift[:, chunk * LANES : (chunk + 1) * LANES]
        for side in range(3):
            local = part + (lane + (1.0 - side) * LANES)
            inside = jnp.logical_and(jnp.logical_and(local >= 0.0, local < LANES), part != 0.0)
            local = jnp.where(inside, local, -1.0).astype(jnp.bfloat16)
            hit = zero
            for slot in range(7):
                hit = jnp.where(row == local[slot : slot + 1, :], one, hit)
            store(chunk + side, chunk, hit)
        store((chunk + 3) % 4, chunk, zero)


def split(value, coeff):
    both = jnp.concatenate([value, coeff * value], axis=0)
    high = both.astype(jnp.bfloat16)
    low = (both - high.astype(jnp.float32)).astype(jnp.bfloat16)
    return high, low


def store_parts(buf, at, parts):
    width = parts[0].shape[1]
    buf[0:112, at : at + width] = parts[0]
    buf[112:224, at : at + width] = parts[1]


def sweep(state, now, later, bases, places):
    first, origin = bases

    def matmul(at, width, matrix):
        low = at - origin - REACH
        return jnp.dot(now[:, low : low + width + 2 * REACH], matrix, preferred_element_type=jnp.float32)

    def finish(at, width, kept, total):
        here = slice(at - first, at - first + width)
        coeff = state[56:57, here]
        value = state[0:56, here]
        change = coeff * (total[0:56] + total[112:168]) + (total[56:112] + total[168:224])
        value = value * (1.0 - change[55:56]) + change
        if kept:
            state[0:56, here] = value
        if later is not None:
            store_parts(later, at - origin, split(value, coeff))

    waiting = None
    for at, width, matrix, kept in places:
        total = matmul(at, width, matrix())
        if waiting is not None:
            finish(*waiting)
        waiting = (at, width, kept, total)
    finish(*waiting)


def interior_blocks(step, count):
    skip = (step + 1) // 2
    return range(skip, count - skip)


def seams(own, side):
    packed = 0
    for step in range(STEPS - 1):
        low = interior_blocks(step, own // BLOCK)[0] * BLOCK
        high = low + REACH + (BLOCK if step % 2 == 0 else 0)
        if side:
            yield step, own - high, own - low, packed
        else:
            yield step, low, high, packed
        packed += high - low


def packed_columns(own):
    return sum(high - low for _, low, high, _ in seams(own, 0))


def interior_kernel(
    head, tail, root, near_adj, far_adj, near_state, far_state, near_parts, far_parts,
    near_values, far_values, near_square, far_square, adj, state, buf0, buf1, buf2, buf3, padded,
):
    bufs = (buf0, buf1, buf2, buf3)
    blocks = adj.shape[0]
    own = blocks * BLOCK
    half = blocks // 2
    for block in range(blocks):
        source, at = (head, block * BLOCK) if block < half else (tail, (block - half) * BLOCK)

        def store(down, across, value):
            spot = (slice(down * LANES, (down + 1) * LANES), slice(across * LANES, (across + 1) * LANES))
            adj[block, *spot] = value
            if block < half:
                near_adj[block, *spot] = value
            if block >= half - 1:
                far_adj[block - (half - 1), *spot] = value

        value = source[:, at : at + BLOCK]
        build_block(value[56:63], store)
        coeff = 0.5 * value[63:64]
        here = block * BLOCK
        state[0:56, here : here + BLOCK] = value[0:56]
        state[56:64, here : here + BLOCK] = jnp.broadcast_to(coeff, (8, BLOCK))
        if block < half - 1:
            near_values[:, here : here + BLOCK] = value[0:56]
        else:
            there = here - (half - 1) * BLOCK
            far_values[:, there : there + BLOCK] = value[0:56]
        store_parts(buf0, here, split(value[0:56], coeff))
    for step in range(1, STEPS - 1):
        whole = interior_blocks(step, blocks)
        places = [(block * BLOCK, BLOCK, functools.partial(lambda b: adj[b], block), True) for block in whole]
        if step % 2:
            low, high = whole[0] - 1, whole[-1] + 1
            places.append((low * BLOCK + REACH, REACH, lambda: adj[low, REACH:, REACH:], False))
            places.append((high * BLOCK, REACH, lambda: adj[high, : BLOCK + REACH, :REACH], False))
        sweep(state, bufs[(step - 1) % 4], bufs[step % 4], (0, 0), places)
    padded[...] = jnp.zeros(padded.shape, jnp.float32)
    padded[0:LEVELS, 0:LEVELS] = root[...]
    matrix = lax.dot_general(
        padded[...], padded[...], (((1,), (1,)), ((), ())),
        precision=lax.Precision.HIGHEST, preferred_element_type=jnp.float32,
    )
    matrix_high = matrix.astype(jnp.bfloat16)
    matrix_low = (matrix - matrix_high.astype(jnp.float32)).astype(jnp.bfloat16)
    near_square[...] = far_square[...] = jnp.concatenate([matrix_high, matrix_low], axis=0)
    near_state[...] = state[:, 0 : own // 2]
    far_state[...] = state[:, own // 2 :]
    for side, parts in ((0, near_parts), (1, far_parts)):
        for step, low, high, packed in seams(own, side):
            parts[:, packed : packed + high - low] = bufs[step % 4][:, low:high]


def load_halo(part, at, state, outer, buf, bases):
    for index in range(HALO // BLOCK):
        value = part[:, index * BLOCK : (index + 1) * BLOCK]
        coeff = 0.5 * value[63:64]
        here = at + index * BLOCK
        spot = slice(here - bases[0], here - bases[0] + BLOCK)
        state[0:56, spot] = value[0:56]
        state[56:64, spot] = jnp.broadcast_to(coeff, (8, BLOCK))
        store_parts(buf, here - bases[1], split(value[0:56], coeff))

        def store(down, across, piece):
            outer[index, down * LANES : (down + 1) * LANES, across * LANES : (across + 1) * LANES] = piece

        build_block(value[56:63], store)


def carry_over(parts, bufs, own, side, bases):
    at = HALO - bases[1]
    for step, low, high, packed in seams(own, side):
        bufs[step % 4][:, at + low : at + high] = parts[:, packed : packed + high - low]


def level_product(square, value):
    high = value.astype(jnp.bfloat16)
    low = (value - high.astype(jnp.float32)).astype(jnp.bfloat16)
    first = jnp.dot(square[...], high, preferred_element_type=jnp.float32)
    second = jnp.dot(square[0:64, :], low, preferred_element_type=jnp.float32)
    return first[0:64] + (first[64:128] + second)


def left_kernel(left, inner, done, parts, values, square, state, seam, outer, buf0, buf1, buf2, buf3):
    own = 2 * done.shape[1]
    bases = (0, -REACH)
    bufs = (buf0, buf1, buf2, buf3)
    fringe = HALO // BLOCK
    middle = fringe + own // BLOCK // 2
    state[:, HALO:] = done[...]
    edge = jnp.zeros((224, REACH), jnp.bfloat16)
    buf0[:, 0:REACH] = edge
    buf2[:, 2 * REACH : 3 * REACH] = edge
    carry_over(parts, bufs, own, 0, bases)
    load_halo(left, 0, state, outer, buf0, bases)
    for step in range(1, STEPS + 1):
        inside = interior_blocks(step, own // BLOCK)
        stop = fringe + inside[0] if len(inside) else middle - (step == STEPS)
        places = [
            (
                block * BLOCK, BLOCK,
                functools.partial(lambda b: outer[b] if b < fringe else inner[b - fringe], block), True,
            )
            for block in range(step // 2, stop)
        ]
        sweep(state, bufs[(step - 1) % 4], bufs[step % 4] if step < STEPS else None, bases, places)
    low = (middle - 1) * BLOCK - REACH - bases[1]
    seam[...] = bufs[(STEPS - 1) % 4][:, low : low + BLOCK + REACH]
    total = jnp.zeros((1, BLOCK), jnp.float32)
    for block in range(own // BLOCK // 2 - 1):
        here = slice(HALO + block * BLOCK, HALO + (block + 1) * BLOCK)
        smoothed = level_product(square, state[:, here])
        state[:, here] = smoothed
        at = block * BLOCK
        total = total + jnp.sum(values[0:LEVELS, at : at + BLOCK] * smoothed[0:LEVELS], axis=0, keepdims=True)
    state[56:57, 0:BLOCK] = total


def right_kernel(
    core, place, right, ens, west, seam, inner, done, parts, values, square,
    keep, send, state, outer, buf0, buf1, buf2, buf3, rowed,
):
    own = 2 * done.shape[1]
    wide = own + 2 * HALO
    tiles = own // LANES
    blocks = wide // BLOCK
    fringe = HALO // BLOCK
    middle = blocks // 2
    bases = ((middle - 1) * BLOCK, (middle - 2) * BLOCK)
    bufs = (buf0, buf1, buf2, buf3)
    state[:, 0:BLOCK] = west[:, (middle - 1) * BLOCK :]
    state[:, BLOCK : BLOCK + own // 2] = done[...]
    edge = jnp.zeros((224, REACH), jnp.bfloat16)
    buf0[:, wide - bases[1] :] = edge
    buf2[:, wide - 2 * REACH - bases[1] : wide - REACH - bases[1]] = edge
    carry_over(parts, bufs, own, 1, bases)
    load_halo(right, HALO + own, state, outer, buf0, bases)
    for step in range(1, STEPS + 1):
        inside = interior_blocks(step, own // BLOCK)
        start = fringe + inside[-1] + 1 if len(inside) else middle - (step == STEPS)
        places = [
            (
                block * BLOCK, BLOCK,
                functools.partial(
                    lambda b: inner[b - (middle - 1)] if b < blocks - fringe else outer[b - (blocks - fringe)], block
                ), True,
            )
            for block in range(start, blocks - step // 2)
        ]
        if step == STEPS:
            low = (middle - 1) * BLOCK - REACH - bases[1]
            bufs[(step - 1) % 4][:, low : low + BLOCK + REACH] = seam[...]
        sweep(state, bufs[(step - 1) % 4], bufs[step % 4] if step < STEPS else None, bases, places)

    total = west[56:57, 0:BLOCK]
    for block in range(own // BLOCK):
        at = (fringe + block) * BLOCK
        if at < bases[0]:
            smoothed = west[0:LEVELS, at : at + BLOCK]
        else:
            smoothed = level_product(square, state[:, at - bases[0] : at - bases[0] + BLOCK])[0:LEVELS]
            there = at - bases[0]
            total = total + jnp.sum(values[0:LEVELS, there : there + BLOCK] * smoothed, axis=0, keepdims=True)
        for tile in range(BLOCK // LANES):
            spot = block * (BLOCK // LANES) + tile
            rowed[pl.ds(spot, LEVELS, stride=tiles), :] = smoothed[:, tile * LANES : (tile + 1) * LANES]
    slots = 4
    chunk = rowed.shape[0] // slots
    spot = pl.ds(slots * chunk, 8)
    keep[spot, :] = send[spot, :] = jnp.broadcast_to(jnp.sum(total, axis=1, keepdims=True), (8, LANES))

    mine, chip = core[0], place[0]
    spare = slots * chunk - LEVELS * tiles

    def products(slot, start, first, count):
        rows = rowed[pl.ds(pl.multiple_of(start + first, 8), count), :]
        at = 2 * (start + first)
        here = pl.ds(slot * chunk + first, count)
        keep[here, :] = ens[pl.ds(at + mine, count, stride=2), :] * rows
        send[here, :] = ens[pl.ds(at + 1 - mine, count, stride=2), :] * rows

    for slot in range(slots):
        target = lax.rem(chip + slot, slots)
        start = target * chunk
        products(slot, start, 0, chunk - spare)

        @pl.when(target < slots - 1)
        def _():
            products(slot, start, chunk - spare, spare)

        @pl.when(target == slots - 1)
        def _():
            nothing = jnp.zeros((spare, LANES), jnp.float32)
            keep[pl.ds((slot + 1) * chunk - spare, spare), :] = nothing
            send[pl.ds((slot + 1) * chunk - spare, spare), :] = nothing


def place_pieces(core, place, slots, same, other, out, lines, sems):
    mine, chip = core[0], place[0]
    chunk = lines.shape[0] // len(slots) // 2
    short = 2 * chunk - (4 * 2 * chunk - out.shape[0])
    waits = []
    for index, slot in enumerate(slots):
        source = lax.rem(chip + 4 - slot, 4)
        start = index * 2 * chunk
        lines[pl.ds(start + mine, chunk, stride=2), :] = same[index, 0:chunk, :]
        lines[pl.ds(start + 1 - mine, chunk, stride=2), :] = other[index, 0:chunk, :]
        target = pl.multiple_of(source * 2 * chunk, 8)
        main = pltpu.make_async_copy(
            lines.at[pl.ds(start, short)], out.at[pl.ds(target, short)], sems.at[0, index]
        )
        extra = pltpu.make_async_copy(
            lines.at[pl.ds(start + short, 2 * chunk - short)],
            out.at[pl.ds(pl.multiple_of(target + short, 8), 2 * chunk - short)],
            sems.at[1, index],
        )
        main.start()
        pl.when(source < 3)(extra.start)
        waits.append((source, main, extra))
    return waits


def wait_pieces(waits):
    for source, main, extra in waits:
        main.wait()
        pl.when(source < 3)(extra.wait)


def early_kernel(scale, core, place, same, other, late, out, quadratic, lines, sems):
    waits = place_pieces(core, place, EARLY, same, other, out, lines, sems)
    chunk = lines.shape[0] // len(EARLY) // 2
    near, far = [
        pieces[0, chunk : chunk + 8, :] + pieces[1, chunk : chunk + 8, :] for pieces in (same, late)
    ]
    quadratic[0, 0] = jnp.max(near + far) * scale
    wait_pieces(waits)


def late_kernel(core, place, begun, same, other, out, lines, sems):
    wait_pieces(place_pieces(core, place, LATE, same, other, out, lines, sems))


def interleave(array):
    cells = array.shape[2]
    array = array.reshape(2, LEVELS, cells // LANES, LANES)
    return array.transpose(1, 2, 0, 3).reshape(-1, LANES)


def on_device(ensemble, field, diffusivity, neighbours, vertical_root):
    own = diffusivity.shape[0]
    patches = lax.axis_size("patch")
    members = lax.axis_size("mem")
    chips = members // 2
    all_cells = own * patches
    half = own // 2
    tiles = own // LANES
    vmem = pl.BlockSpec(memory_space=pltpu.VMEM)
    smem = pl.BlockSpec(memory_space=pltpu.SMEM)
    hbm = pl.BlockSpec(memory_space=pltpu.HBM)
    params = pltpu.CompilerParams(vmem_limit_bytes=32 * 1024 * 1024)
    place = (lax.axis_index("patch") * own).astype(jnp.int32).reshape(1)
    member = lax.axis_index("mem")
    ids = [
        jnp.bitwise_and(member, 1).astype(jnp.int32).reshape(1),
        lax.shift_right_logical(member, 1).astype(jnp.int32).reshape(1),
    ]
    ens_rows = interleave(ensemble[0])
    field_rows = interleave(field)

    in_hbm = [
        pltpu.with_memory_space_constraint(array, pltpu.HBM)
        for array in (
            ens_rows.reshape(LEVELS, 2 * tiles, LANES),
            field_rows.reshape(LEVELS, 2 * tiles, LANES),
            diffusivity.reshape(1, own),
            neighbours,
        )
    ]
    tail, head = [
        pl.pallas_call(
            functools.partial(prepare_kernel, all_cells, part),
            out_shape=jax.ShapeDtypeStruct((64, half), jnp.float32),
            in_specs=[smem, hbm, hbm, hbm, hbm],
            out_specs=vmem,
            scratch_shapes=[
                pltpu.VMEM((LEVELS, tiles, LANES), jnp.float32),
                pltpu.VMEM((LEVELS, tiles, LANES), jnp.float32),
                pltpu.VMEM((1, half), jnp.float32),
                pltpu.VMEM((7, half), jnp.int32),
                pltpu.SemaphoreType.DMA((3, 4)),
            ],
            compiler_params=params,
            name=name,
        )(place, *in_hbm)
        for part, name in ((1, "tail"), (0, "head"))
    ]

    left = lax.ppermute(tail, "patch", [(i, (i + 1) % patches) for i in range(patches)])
    right = lax.ppermute(head, "patch", [((i + 1) % patches, i) for i in range(patches)])

    blocks = own // BLOCK
    adjacency = (2 * BLOCK, BLOCK)
    packed = jax.ShapeDtypeStruct((224, packed_columns(own)), jnp.bfloat16)
    half_state = jax.ShapeDtypeStruct((64, half), jnp.float32)
    squared = jax.ShapeDtypeStruct((128, 64), jnp.bfloat16)
    inside = pl.pallas_call(
        interior_kernel,
        out_shape=(
            jax.ShapeDtypeStruct((blocks // 2, *adjacency), jnp.bfloat16),
            jax.ShapeDtypeStruct((blocks // 2 + 1, *adjacency), jnp.bfloat16),
            half_state, half_state, packed, packed,
            jax.ShapeDtypeStruct((56, half - BLOCK), jnp.float32),
            jax.ShapeDtypeStruct((56, half + BLOCK), jnp.float32),
            squared, squared,
        ),
        in_specs=[vmem] * 3,
        out_specs=(vmem,) * 10,
        scratch_shapes=[pltpu.VMEM((blocks, *adjacency), jnp.bfloat16), pltpu.VMEM((64, own), jnp.float32)]
        + [pltpu.VMEM((224, own), jnp.bfloat16)] * 4
        + [pltpu.VMEM((64, 64), jnp.float32)],
        compiler_params=params,
        cost_estimate=pl.CostEstimate(flops=4_000_000_000, bytes_accessed=4_000_000, transcendentals=0),
        name="interior",
    )(head, tail, vertical_root)

    chunk = 56 * tiles // chips
    west, seam = pl.pallas_call(
        left_kernel,
        out_shape=(
            jax.ShapeDtypeStruct((64, HALO + half), jnp.float32),
            jax.ShapeDtypeStruct((224, BLOCK + REACH), jnp.bfloat16),
        ),
        in_specs=[vmem] * 6,
        out_specs=(vmem,) * 2,
        scratch_shapes=[pltpu.VMEM((HALO // BLOCK, 2 * BLOCK, BLOCK), jnp.bfloat16)]
        + [pltpu.VMEM((224, HALO + half + 2 * REACH), jnp.bfloat16)] * 4,
        compiler_params=params,
        cost_estimate=pl.CostEstimate(flops=0, bytes_accessed=7_000_000, transcendentals=0),
        name="left",
    )(left, *inside[0::2])
    terms = jax.ShapeDtypeStruct((chips * chunk + 8, LANES), jnp.float32)
    keep, send = pl.pallas_call(
        right_kernel,
        out_shape=(terms, terms),
        in_specs=[smem] * 2 + [vmem] * 9,
        out_specs=(vmem, vmem),
        scratch_shapes=[
            pltpu.VMEM((64, BLOCK + half + HALO), jnp.float32),
            pltpu.VMEM((HALO // BLOCK, 2 * BLOCK, BLOCK), jnp.bfloat16),
        ]
        + [pltpu.VMEM((224, 2 * BLOCK + half + HALO + REACH), jnp.bfloat16)] * 4
        + [pltpu.VMEM((56 * tiles, LANES), jnp.float32)],
        compiler_params=params,
        cost_estimate=pl.CostEstimate(flops=0, bytes_accessed=7_000_000, transcendentals=0),
        name="right",
    )(*ids, right, ens_rows, west, seam, *inside[1::2])

    def shift_chips(array, by):
        pairs = [(2 * z + c, 2 * ((z + by) % chips) + c) for z in range(chips) for c in range(2)]
        return lax.ppermute(array, "mem", pairs)

    twin = [(i, i ^ 1) for i in range(members)]
    order = [2, 1, 3]
    pair_sum = keep + lax.ppermute(send, "mem", twin)
    pieces = [pair_sum[chunk * slot : chunk * (slot + 1)] for slot in range(chips)]
    terms = {by: shift_chips(pieces[by], by) for by in order}
    spread = jnp.broadcast_to(pair_sum[chips * chunk : chips * chunk + 1][None], (patches, 1, LANES))
    spread = lax.all_to_all(spread, "patch", 0, 0)
    terms, spread = lax.optimization_barrier((terms, spread))
    total = (pieces[0] + terms[1] + terms[2] + terms[3]) / (members - 1.0)
    total = jnp.concatenate([total, jnp.broadcast_to(jnp.sum(spread, axis=0), (8, LANES))], axis=0)
    copies = {by: shift_chips(total, by) for by in order}
    sources = {0: total, **copies}
    scale = 1.0 / ((members - 1.0) * field.shape[0] * field.shape[1] * all_cells)
    scratch = [
        pltpu.VMEM((2 * chunk * 2, LANES), jnp.float32),
        pltpu.SemaphoreType.DMA((2, 2)),
    ]
    early = jnp.stack([sources[by] for by in EARLY])
    late = jnp.stack([sources[by] for by in LATE])
    rows, quadratic = pl.pallas_call(
        functools.partial(early_kernel, scale),
        out_shape=(
            jax.ShapeDtypeStruct(field_rows.shape, jnp.float32),
            jax.ShapeDtypeStruct((1, 1), jnp.float32),
        ),
        in_specs=[smem, smem, vmem, vmem, vmem],
        out_specs=(hbm, smem),
        scratch_shapes=scratch,
        compiler_params=params,
        cost_estimate=pl.CostEstimate(flops=1_000_000, bytes_accessed=4_000_000, transcendentals=0),
        name="early",
    )(*ids, early, lax.ppermute(early, "mem", twin), late)
    rows = pl.pallas_call(
        late_kernel,
        out_shape=jax.ShapeDtypeStruct(field_rows.shape, jnp.float32),
        in_specs=[smem, smem, hbm, vmem, vmem],
        out_specs=hbm,
        scratch_shapes=scratch,
        input_output_aliases={2: 0},
        compiler_params=params,
        name="late",
    )(*ids, rows, late, lax.ppermute(late, "mem", twin))
    product = rows.reshape(LEVELS, tiles, 2, LANES).transpose(2, 0, 1, 3).reshape(field.shape)
    return (product, quadratic.reshape(()))


def solution(mesh):
    return jax.shard_map(
        on_device,
        mesh=mesh,
        in_specs=(
            P("mem", None, None, "patch"),
            P(None, None, "patch"),
            P("patch"),
            P(None, "patch"),
            P(),
        ),
        out_specs=(P(None, None, "patch"), P()),
        check_vma=False,
    )
```

```python
import functools

import jax
import jax.numpy as jnp
from jax import lax
from jax.experimental import pallas as pl
from jax.experimental.pallas import tpu as pltpu
from jax.sharding import PartitionSpec as P

STEPS = 8
REACH = 128
BLOCK = 256
HALO = STEPS * REACH
LEVELS = 55
LANES = 128
EARLY, LATE = (0, 2), (1, 3)


def prepare_kernel(
    all_cells, place, ens, field, diff, neigh, head, tail, ens_in, field_in, diff_in, neigh_in, sems
):
    own = diff.shape[1]
    tiles = own // LANES
    half = own // 2
    start = place[0]
    levels = (0, 16, 32, 48, LEVELS)
    copies = []
    for turn in range(4):
        rows = pl.ds(levels[turn] * 2 * tiles, (levels[turn + 1] - levels[turn]) * 2 * tiles)
        copies.append((
            pltpu.make_async_copy(ens.at[rows], ens_in.at[rows], sems.at[0, turn]),
            pltpu.make_async_copy(field.at[rows], field_in.at[rows], sems.at[1, turn]),
        ))
    others = (
        pltpu.make_async_copy(neigh, neigh_in, sems.at[2, 0]),
        pltpu.make_async_copy(diff, diff_in, sems.at[2, 1]),
    )
    for copy in others + copies[0] + copies[1] + copies[2] + copies[3]:
        copy.start()
    for copy in others:
        copy.wait()
    for part, out in ((0, head), (1, tail)):
        cols = pl.ds(part * half, half)
        out[55:56, :] = jnp.ones((1, half), jnp.float32)
        cell = lax.broadcasted_iota(jnp.int32, (7, half), 1) + (start + part * half)
        shift = neigh_in[:, cols] - cell
        shift = jnp.where(shift > all_cells // 2, shift - all_cells, shift)
        shift = jnp.where(shift < -(all_cells // 2), shift + all_cells, shift)
        out[56:63, :] = shift.astype(jnp.float32)
        out[63:64, :] = diff_in[:, cols]
    for turn in range(4):
        for copy in copies[turn]:
            copy.wait()
        low, high = levels[turn], levels[turn + 1]
        rows = pl.ds(low * 2 * tiles, (high - low) * 2 * tiles)
        ens_in[rows, :] = ens_in[rows, :] * field_in[rows, :]
        for part, out in ((0, head), (1, tail)):
            for tile in range(tiles // 2):
                at = low * 2 * tiles + 2 * (part * (tiles // 2) + tile)
                out[low:high, tile * LANES : (tile + 1) * LANES] = (
                    ens_in[pl.ds(at, high - low, stride=2 * tiles), :]
                    + ens_in[pl.ds(at + 1, high - low, stride=2 * tiles), :]
                )


def build_block(shift, store):
    row = lax.broadcasted_iota(jnp.int32, (LANES, LANES), 0).astype(jnp.float32).astype(jnp.bfloat16)
    lane = lax.broadcasted_iota(jnp.int32, (1, LANES), 1).astype(jnp.float32)
    one = jnp.ones((LANES, LANES), jnp.bfloat16)
    zero = jnp.zeros((LANES, LANES), jnp.bfloat16)
    for chunk in range(BLOCK // LANES):
        part = shift[:, chunk * LANES : (chunk + 1) * LANES]
        for side in range(3):
            local = part + (lane + (1.0 - side) * LANES)
            inside = jnp.logical_and(jnp.logical_and(local >= 0.0, local < LANES), part != 0.0)
            local = jnp.where(inside, local, -1.0).astype(jnp.bfloat16)
            hit = zero
            for slot in range(7):
                hit = jnp.where(row == local[slot : slot + 1, :], one, hit)
            store(chunk + side, chunk, hit)
        store((chunk + 3) % 4, chunk, zero)


def split(value, coeff):
    both = jnp.concatenate([value, coeff * value], axis=0)
    high = both.astype(jnp.bfloat16)
    low = (both - high.astype(jnp.float32)).astype(jnp.bfloat16)
    return high, low


def store_parts(buf, at, parts):
    width = parts[0].shape[1]
    buf[0:112, at : at + width] = parts[0]
    buf[112:224, at : at + width] = parts[1]


def sweep(state, now, later, bases, places):
    first, origin = bases

    def matmul(at, width, matrix):
        low = at - origin - REACH
        return jnp.dot(now[:, low : low + width + 2 * REACH], matrix, preferred_element_type=jnp.float32)

    def finish(at, width, kept, total):
        here = slice(at - first, at - first + width)
        coeff = state[56:57, here]
        value = state[0:56, here]
        change = coeff * (total[0:56] + total[112:168]) + (total[56:112] + total[168:224])
        value = value * (1.0 - change[55:56]) + change
        if kept:
            state[0:56, here] = value
        if later is not None:
            store_parts(later, at - origin, split(value, coeff))

    waiting = None
    for at, width, matrix, kept in places:
        total = matmul(at, width, matrix())
        if waiting is not None:
            finish(*waiting)
        waiting = (at, width, kept, total)
    finish(*waiting)


def interior_blocks(step, count):
    skip = (step + 1) // 2
    return range(skip, count - skip)


def seams(own, side):
    packed = 0
    for step in range(STEPS - 1):
        low = interior_blocks(step, own // BLOCK)[0] * BLOCK
        high = low + REACH + (BLOCK if step % 2 == 0 else 0)
        if side:
            yield step, own - high, own - low, packed
        else:
            yield step, low, high, packed
        packed += high - low


def packed_columns(own):
    return sum(high - low for _, low, high, _ in seams(own, 0))


def interior_kernel(
    head, tail, root, near_adj, far_adj, near_state, far_state, near_parts, far_parts,
    near_values, far_values, near_square, far_square, adj, state, buf0, buf1, buf2, buf3, padded,
):
    bufs = (buf0, buf1, buf2, buf3)
    blocks = adj.shape[0]
    own = blocks * BLOCK
    half = blocks // 2
    for block in range(blocks):
        source, at = (head, block * BLOCK) if block < half else (tail, (block - half) * BLOCK)

        def store(down, across, value):
            spot = (slice(down * LANES, (down + 1) * LANES), slice(across * LANES, (across + 1) * LANES))
            adj[block, *spot] = value
            if block < half:
                near_adj[block, *spot] = value
            if block >= half - 1:
                far_adj[block - (half - 1), *spot] = value

        value = source[:, at : at + BLOCK]
        build_block(value[56:63], store)
        coeff = 0.5 * value[63:64]
        here = block * BLOCK
        state[0:56, here : here + BLOCK] = value[0:56]
        state[56:64, here : here + BLOCK] = jnp.broadcast_to(coeff, (8, BLOCK))
        if block < half - 1:
            near_values[:, here : here + BLOCK] = value[0:56]
        else:
            there = here - (half - 1) * BLOCK
            far_values[:, there : there + BLOCK] = value[0:56]
        store_parts(buf0, here, split(value[0:56], coeff))
    for step in range(1, STEPS - 1):
        whole = interior_blocks(step, blocks)
        places = [(block * BLOCK, BLOCK, functools.partial(lambda b: adj[b], block), True) for block in whole]
        if step % 2:
            low, high = whole[0] - 1, whole[-1] + 1
            places.append((low * BLOCK + REACH, REACH, lambda: adj[low, REACH:, REACH:], False))
            places.append((high * BLOCK, REACH, lambda: adj[high, : BLOCK + REACH, :REACH], False))
        sweep(state, bufs[(step - 1) % 4], bufs[step % 4], (0, 0), places)
    padded[...] = jnp.zeros(padded.shape, jnp.float32)
    padded[0:LEVELS, 0:LEVELS] = root[...]
    matrix = lax.dot_general(
        padded[...], padded[...], (((1,), (1,)), ((), ())),
        precision=lax.Precision.HIGHEST, preferred_element_type=jnp.float32,
    )
    matrix_high = matrix.astype(jnp.bfloat16)
    matrix_low = (matrix - matrix_high.astype(jnp.float32)).astype(jnp.bfloat16)
    near_square[...] = far_square[...] = jnp.concatenate([matrix_high, matrix_low], axis=0)
    near_state[...] = state[:, 0 : own // 2]
    far_state[...] = state[:, own // 2 :]
    for side, parts in ((0, near_parts), (1, far_parts)):
        for step, low, high, packed in seams(own, side):
            parts[:, packed : packed + high - low] = bufs[step % 4][:, low:high]


def load_halo(part, at, state, outer, buf, bases):
    for index in range(HALO // BLOCK):
        value = part[:, index * BLOCK : (index + 1) * BLOCK]
        coeff = 0.5 * value[63:64]
        here = at + index * BLOCK
        spot = slice(here - bases[0], here - bases[0] + BLOCK)
        state[0:56, spot] = value[0:56]
        state[56:64, spot] = jnp.broadcast_to(coeff, (8, BLOCK))
        store_parts(buf, here - bases[1], split(value[0:56], coeff))

        def store(down, across, piece):
            outer[index, down * LANES : (down + 1) * LANES, across * LANES : (across + 1) * LANES] = piece

        build_block(value[56:63], store)


def carry_over(parts, bufs, own, side, bases):
    at = HALO - bases[1]
    for step, low, high, packed in seams(own, side):
        bufs[step % 4][:, at + low : at + high] = parts[:, packed : packed + high - low]


def level_product(square, value):
    high = value.astype(jnp.bfloat16)
    low = (value - high.astype(jnp.float32)).astype(jnp.bfloat16)
    first = jnp.dot(square[...], high, preferred_element_type=jnp.float32)
    second = jnp.dot(square[0:64, :], low, preferred_element_type=jnp.float32)
    return first[0:64] + (first[64:128] + second)


def left_kernel(left, inner, done, parts, values, square, state, seam, outer, buf0, buf1, buf2, buf3):
    own = 2 * done.shape[1]
    bases = (0, -REACH)
    bufs = (buf0, buf1, buf2, buf3)
    fringe = HALO // BLOCK
    middle = fringe + own // BLOCK // 2
    state[:, HALO:] = done[...]
    edge = jnp.zeros((224, REACH), jnp.bfloat16)
    buf0[:, 0:REACH] = edge
    buf2[:, 2 * REACH : 3 * REACH] = edge
    carry_over(parts, bufs, own, 0, bases)
    load_halo(left, 0, state, outer, buf0, bases)
    for step in range(1, STEPS + 1):
        inside = interior_blocks(step, own // BLOCK)
        stop = fringe + inside[0] if len(inside) else middle - (step == STEPS)
        places = [
            (
                block * BLOCK, BLOCK,
                functools.partial(lambda b: outer[b] if b < fringe else inner[b - fringe], block), True,
            )
            for block in range(step // 2, stop)
        ]
        if step % 2:
            at, matrix = places[0][0] + REACH, functools.partial(lambda b: outer[b, REACH:, REACH:], step // 2)
            places[0] = (at, REACH, matrix, True)
        sweep(state, bufs[(step - 1) % 4], bufs[step % 4] if step < STEPS else None, bases, places)
    low = (middle - 1) * BLOCK - REACH - bases[1]
    seam[...] = bufs[(STEPS - 1) % 4][:, low : low + BLOCK + REACH]
    total = jnp.zeros((1, BLOCK), jnp.float32)
    for block in range(own // BLOCK // 2 - 1):
        here = slice(HALO + block * BLOCK, HALO + (block + 1) * BLOCK)
        smoothed = level_product(square, state[:, here])
        state[:, here] = smoothed
        at = block * BLOCK
        total = total + jnp.sum(values[0:LEVELS, at : at + BLOCK] * smoothed[0:LEVELS], axis=0, keepdims=True)
    state[56:57, 0:BLOCK] = total


def right_kernel(
    core, place, right, ens, west, seam, inner, done, parts, values, square,
    keep, send, state, outer, buf0, buf1, buf2, buf3, rowed,
):
    own = 2 * done.shape[1]
    wide = own + 2 * HALO
    tiles = own // LANES
    blocks = wide // BLOCK
    fringe = HALO // BLOCK
    middle = blocks // 2
    bases = ((middle - 1) * BLOCK, (middle - 2) * BLOCK)
    bufs = (buf0, buf1, buf2, buf3)
    state[:, 0:BLOCK] = west[:, (middle - 1) * BLOCK :]
    state[:, BLOCK : BLOCK + own // 2] = done[...]
    edge = jnp.zeros((224, REACH), jnp.bfloat16)
    buf0[:, wide - bases[1] :] = edge
    buf2[:, wide - 2 * REACH - bases[1] : wide - REACH - bases[1]] = edge
    carry_over(parts, bufs, own, 1, bases)
    load_halo(right, HALO + own, state, outer, buf0, bases)
    for step in range(1, STEPS + 1):
        inside = interior_blocks(step, own // BLOCK)
        start = fringe + inside[-1] + 1 if len(inside) else middle - (step == STEPS)
        places = [
            (
                block * BLOCK, BLOCK,
                functools.partial(
                    lambda b: inner[b - (middle - 1)] if b < blocks - fringe else outer[b - (blocks - fringe)], block
                ), True,
            )
            for block in range(start, blocks - step // 2)
        ]
        if step % 2:
            matrix = functools.partial(lambda b: outer[b, : BLOCK + REACH, :REACH], fringe - 1 - step // 2)
            places[-1] = (places[-1][0], REACH, matrix, True)
        if step == STEPS:
            low = (middle - 1) * BLOCK - REACH - bases[1]
            bufs[(step - 1) % 4][:, low : low + BLOCK + REACH] = seam[...]
        sweep(state, bufs[(step - 1) % 4], bufs[step % 4] if step < STEPS else None, bases, places)

    total = west[56:57, 0:BLOCK]
    for block in range(own // BLOCK):
        at = (fringe + block) * BLOCK
        if at < bases[0]:
            smoothed = west[0:LEVELS, at : at + BLOCK]
        else:
            smoothed = level_product(square, state[:, at - bases[0] : at - bases[0] + BLOCK])[0:LEVELS]
            there = at - bases[0]
            total = total + jnp.sum(values[0:LEVELS, there : there + BLOCK] * smoothed, axis=0, keepdims=True)
        for tile in range(BLOCK // LANES):
            spot = block * (BLOCK // LANES) + tile
            rowed[pl.ds(spot, LEVELS, stride=tiles), :] = smoothed[:, tile * LANES : (tile + 1) * LANES]
    slots = 4
    chunk = rowed.shape[0] // slots
    spot = pl.ds(slots * chunk, 8)
    keep[spot, :] = send[spot, :] = jnp.broadcast_to(jnp.sum(total, axis=1, keepdims=True), (8, LANES))

    mine, chip = core[0], place[0]
    spare = slots * chunk - LEVELS * tiles

    def products(slot, start, first, count):
        rows = rowed[pl.ds(pl.multiple_of(start + first, 8), count), :]
        at = 2 * (start + first)
        here = pl.ds(slot * chunk + first, count)
        keep[here, :] = ens[pl.ds(at + mine, count, stride=2), :] * rows
        send[here, :] = ens[pl.ds(at + 1 - mine, count, stride=2), :] * rows

    for slot in range(slots):
        target = lax.rem(chip + slot, slots)
        start = target * chunk
        products(slot, start, 0, chunk - spare)

        @pl.when(target < slots - 1)
        def _():
            products(slot, start, chunk - spare, spare)

        @pl.when(target == slots - 1)
        def _():
            nothing = jnp.zeros((spare, LANES), jnp.float32)
            keep[pl.ds((slot + 1) * chunk - spare, spare), :] = nothing
            send[pl.ds((slot + 1) * chunk - spare, spare), :] = nothing


def place_pieces(core, place, slots, same, other, out, lines, sems):
    mine, chip = core[0], place[0]
    chunk = lines.shape[0] // len(slots) // 2
    short = 2 * chunk - (4 * 2 * chunk - out.shape[0])
    waits = []
    for index, slot in enumerate(slots):
        source = lax.rem(chip + 4 - slot, 4)
        start = index * 2 * chunk
        lines[pl.ds(start + mine, chunk, stride=2), :] = same[index, 0:chunk, :]
        lines[pl.ds(start + 1 - mine, chunk, stride=2), :] = other[index, 0:chunk, :]
        target = pl.multiple_of(source * 2 * chunk, 8)
        main = pltpu.make_async_copy(
            lines.at[pl.ds(start, short)], out.at[pl.ds(target, short)], sems.at[0, index]
        )
        extra = pltpu.make_async_copy(
            lines.at[pl.ds(start + short, 2 * chunk - short)],
            out.at[pl.ds(pl.multiple_of(target + short, 8), 2 * chunk - short)],
            sems.at[1, index],
        )
        main.start()
        pl.when(source < 3)(extra.start)
        waits.append((source, main, extra))
    return waits


def wait_pieces(waits):
    for source, main, extra in waits:
        main.wait()
        pl.when(source < 3)(extra.wait)


def early_kernel(core, place, same, other, out, lines, sems):
    wait_pieces(place_pieces(core, place, EARLY, same, other, out, lines, sems))


def late_kernel(scale, core, place, begun, early, same, other, out, quadratic, lines, sems):
    waits = place_pieces(core, place, LATE, same, other, out, lines, sems)
    chunk = lines.shape[0] // len(LATE) // 2
    near, far = [
        pieces[0, chunk : chunk + 8, :] + pieces[1, chunk : chunk + 8, :] for pieces in (early, same)
    ]
    quadratic[0, 0] = jnp.max(near + far) * scale
    wait_pieces(waits)


def interleave(array):
    cells = array.shape[2]
    array = array.reshape(2, LEVELS, cells // LANES, LANES)
    return array.transpose(1, 2, 0, 3).reshape(-1, LANES)


def on_device(ensemble, field, diffusivity, neighbours, vertical_root):
    own = diffusivity.shape[0]
    patches = lax.axis_size("patch")
    members = lax.axis_size("mem")
    chips = members // 2
    all_cells = own * patches
    half = own // 2
    tiles = own // LANES
    vmem = pl.BlockSpec(memory_space=pltpu.VMEM)
    smem = pl.BlockSpec(memory_space=pltpu.SMEM)
    hbm = pl.BlockSpec(memory_space=pltpu.HBM)
    params = pltpu.CompilerParams(vmem_limit_bytes=32 * 1024 * 1024)
    place = (lax.axis_index("patch") * own).astype(jnp.int32).reshape(1)
    member = lax.axis_index("mem")
    ids = [
        jnp.bitwise_and(member, 1).astype(jnp.int32).reshape(1),
        lax.shift_right_logical(member, 1).astype(jnp.int32).reshape(1),
    ]
    ens_rows = interleave(ensemble[0])
    field_rows = interleave(field)

    in_hbm = [
        pltpu.with_memory_space_constraint(array, pltpu.HBM)
        for array in (ens_rows, field_rows, diffusivity.reshape(1, own), neighbours)
    ]
    side = jax.ShapeDtypeStruct((64, half), jnp.float32)
    head, tail = pl.pallas_call(
        functools.partial(prepare_kernel, all_cells),
        out_shape=(side, side),
        in_specs=[smem, hbm, hbm, hbm, hbm],
        out_specs=(vmem, vmem),
        scratch_shapes=[
            pltpu.VMEM(ens_rows.shape, jnp.float32),
            pltpu.VMEM(ens_rows.shape, jnp.float32),
            pltpu.VMEM((1, own), jnp.float32),
            pltpu.VMEM((7, own), jnp.int32),
            pltpu.SemaphoreType.DMA((3, 4)),
        ],
        compiler_params=params,
        name="prepare",
    )(place, *in_hbm)

    left = lax.ppermute(tail, "patch", [(i, (i + 1) % patches) for i in range(patches)])
    right = lax.ppermute(head, "patch", [((i + 1) % patches, i) for i in range(patches)])

    blocks = own // BLOCK
    adjacency = (2 * BLOCK, BLOCK)
    packed = jax.ShapeDtypeStruct((224, packed_columns(own)), jnp.bfloat16)
    half_state = jax.ShapeDtypeStruct((64, half), jnp.float32)
    squared = jax.ShapeDtypeStruct((128, 64), jnp.bfloat16)
    inside = pl.pallas_call(
        interior_kernel,
        out_shape=(
            jax.ShapeDtypeStruct((blocks // 2, *adjacency), jnp.bfloat16),
            jax.ShapeDtypeStruct((blocks // 2 + 1, *adjacency), jnp.bfloat16),
            half_state, half_state, packed, packed,
            jax.ShapeDtypeStruct((56, half - BLOCK), jnp.float32),
            jax.ShapeDtypeStruct((56, half + BLOCK), jnp.float32),
            squared, squared,
        ),
        in_specs=[vmem] * 3,
        out_specs=(vmem,) * 10,
        scratch_shapes=[pltpu.VMEM((blocks, *adjacency), jnp.bfloat16), pltpu.VMEM((64, own), jnp.float32)]
        + [pltpu.VMEM((224, own), jnp.bfloat16)] * 4
        + [pltpu.VMEM((64, 64), jnp.float32)],
        compiler_params=params,
        cost_estimate=pl.CostEstimate(flops=4_000_000_000, bytes_accessed=4_000_000, transcendentals=0),
        name="interior",
    )(head, tail, vertical_root)

    chunk = 56 * tiles // chips
    west, seam = pl.pallas_call(
        left_kernel,
        out_shape=(
            jax.ShapeDtypeStruct((64, HALO + half), jnp.float32),
            jax.ShapeDtypeStruct((224, BLOCK + REACH), jnp.bfloat16),
        ),
        in_specs=[vmem] * 6,
        out_specs=(vmem,) * 2,
        scratch_shapes=[pltpu.VMEM((HALO // BLOCK, 2 * BLOCK, BLOCK), jnp.bfloat16)]
        + [pltpu.VMEM((224, HALO + half + 2 * REACH), jnp.bfloat16)] * 4,
        compiler_params=params,
        cost_estimate=pl.CostEstimate(flops=0, bytes_accessed=7_000_000, transcendentals=0),
        name="left",
    )(left, *inside[0::2])
    terms = jax.ShapeDtypeStruct((chips * chunk + 8, LANES), jnp.float32)
    keep, send = pl.pallas_call(
        right_kernel,
        out_shape=(terms, terms),
        in_specs=[smem] * 2 + [vmem] * 9,
        out_specs=(vmem, vmem),
        scratch_shapes=[
            pltpu.VMEM((64, BLOCK + half + HALO), jnp.float32),
            pltpu.VMEM((HALO // BLOCK, 2 * BLOCK, BLOCK), jnp.bfloat16),
        ]
        + [pltpu.VMEM((224, 2 * BLOCK + half + HALO + REACH), jnp.bfloat16)] * 4
        + [pltpu.VMEM((56 * tiles, LANES), jnp.float32)],
        compiler_params=params,
        cost_estimate=pl.CostEstimate(flops=0, bytes_accessed=7_000_000, transcendentals=0),
        name="right",
    )(*ids, right, ens_rows, west, seam, *inside[1::2])

    def shift_chips(array, by):
        pairs = [(2 * z + c, 2 * ((z + by) % chips) + c) for z in range(chips) for c in range(2)]
        return lax.ppermute(array, "mem", pairs)

    twin = [(i, i ^ 1) for i in range(members)]
    order = [2, 1, 3]
    pair_sum = keep + lax.ppermute(send, "mem", twin)
    pieces = [pair_sum[chunk * slot : chunk * (slot + 1)] for slot in range(chips)]
    terms = {by: shift_chips(pieces[by], by) for by in order}
    spread = jnp.broadcast_to(pair_sum[chips * chunk : chips * chunk + 1][None], (patches, 1, LANES))
    spread = lax.all_to_all(spread, "patch", 0, 0)
    terms, spread = lax.optimization_barrier((terms, spread))
    total = (pieces[0] + terms[1] + terms[2] + terms[3]) / (members - 1.0)
    total = jnp.concatenate([total, jnp.broadcast_to(jnp.sum(spread, axis=0), (8, LANES))], axis=0)
    copies = {by: shift_chips(total, by) for by in order}
    sources = {0: total, **copies}
    scale = 1.0 / ((members - 1.0) * field.shape[0] * field.shape[1] * all_cells)
    scratch = [
        pltpu.VMEM((2 * chunk * 2, LANES), jnp.float32),
        pltpu.SemaphoreType.DMA((2, 2)),
    ]
    early = jnp.stack([sources[by] for by in EARLY])
    rows = pl.pallas_call(
        early_kernel,
        out_shape=jax.ShapeDtypeStruct(field_rows.shape, jnp.float32),
        in_specs=[smem, smem, vmem, vmem],
        out_specs=hbm,
        scratch_shapes=scratch,
        compiler_params=params,
        cost_estimate=pl.CostEstimate(flops=1_000_000, bytes_accessed=4_000_000, transcendentals=0),
        name="early",
    )(*ids, early, lax.ppermute(early, "mem", twin))
    late = jnp.stack([sources[by] for by in LATE])
    rows, quadratic = pl.pallas_call(
        functools.partial(late_kernel, scale),
        out_shape=(
            jax.ShapeDtypeStruct(field_rows.shape, jnp.float32),
            jax.ShapeDtypeStruct((1, 1), jnp.float32),
        ),
        in_specs=[smem, smem, hbm, vmem, vmem, vmem],
        out_specs=(hbm, smem),
        scratch_shapes=scratch,
        input_output_aliases={2: 0},
        compiler_params=params,
        name="late",
    )(*ids, rows, early, late, lax.ppermute(late, "mem", twin))
    product = rows.reshape(LEVELS, tiles, 2, LANES).transpose(2, 0, 1, 3).reshape(field.shape)
    return (product, quadratic.reshape(()))


def solution(mesh):
    return jax.shard_map(
        on_device,
        mesh=mesh,
        in_specs=(
            P("mem", None, None, "patch"),
            P(None, None, "patch"),
            P("patch"),
            P(None, "patch"),
            P(),
        ),
        out_specs=(P(None, None, "patch"), P()),
        check_vma=False,
    )
```
